512 devices in a mesh: win: 32 (over y_lo, z), head: 16 (over x, y_hi, core).
Axes of the slice: x: 4, y: 8 (y_hi: 2, y_lo: 4; y = y_hi * 4 + y_lo), z: 8, core: 2. Of those that a mesh axis runs over, the one named last changes fastest.
Arguments:
- latents: bfloat16 [32, 8, 128, 3072], P('win', None, 'head'), may hold values from -6 to 6
- prompt_ids: int32 [32], P('win'), may hold values from 0 to 7
- modulation: float32 [8, 3, 3072], replicated, may hold values from -2.5 to 5
- w_qkv: bfloat16 [3, 3072, 3072], P(None, 'head'), may hold values from -0.5 to 0.5
- intersection: int32 [32], replicated, may hold values from 0 to 3, as said below
Outputs:
- blended: bfloat16 [32, 8, 128, 3072], P('win', None, 'head')
The draws below stay inside these ranges and needn't reach their ends.
Inputs may be any that keep to these rules, and one draw needn't show every extreme that they name: intersection[0] is 0; every other entry lies in 1 to 3, and some entry equals 3.
All inputs are finite; a program needn't handle non-finite values.
Results may differ from the reference program's by a relative error of at most 0.024.
The reference program's roundings to bfloat16 on the way (of `normed`, `qkv`, `probs`, `attended` and `averaged`) count: a program that leaves them out, or rounds other values in their place, can miss the bound.
Values may be sent and summed in bfloat16 or wider, within the bound.
No kernel may reach another device: no remote copies, remote signals or barrier semaphores. Data moves between devices by JAX's collectives and lax.ppermute only.
A program may use at most 64 MiB of HBM per device.

```python
import jax
import jax.numpy as jnp
from jax import lax

D = 3072
HEADS = 48
HEAD_DIM = 64
WF = 8
OMAX = 3
PROMPTS = 8
P_SIZE = 128
WINS = 32


def draw_modulation(key, part):
    key = jax.random.fold_in(key, 11)
    key_shift, key_scale, key_gate = jax.random.split(key, 3)
    shape = (PROMPTS, 1, D)
    shift = jnp.clip(0.5 * jax.random.normal(key_shift, shape, jnp.float32), -1.5, 1.5)
    scale = jnp.clip(0.3 * jax.random.normal(key_scale, shape, jnp.float32), -0.9, 1.0)
    gate = jnp.clip(jax.random.normal(key_gate, shape, jnp.float32), -2.5, 2.5)
    return jnp.concatenate([shift, scale, gate], axis=1)


def draw_intersection(key, part):
    key = jax.random.fold_in(key, 5)
    key_vals, key_pick = jax.random.split(key)
    values = jax.random.randint(key_vals, (WINS,), 1, OMAX + 1, dtype=jnp.int32)
    chosen = jax.random.randint(key_pick, (), 1, WINS, dtype=jnp.int32)
    positions = jnp.arange(WINS, dtype=jnp.int32)
    values = jnp.where(positions == chosen, OMAX, values)
    values = jnp.where(positions == 0, 0, values)
    return values.astype(jnp.int32)


def touch_ends(entries, rng, smallest, largest):
    extent = entries.shape
    index_at = [jax.random.randint(jax.random.fold_in(rng, axis), (), 0, extent[axis]) for axis in range(len(extent))]
    entries = entries.at[tuple(index_at)].set(smallest)
    longest = extent.index(max(extent))
    index_at[longest] = (index_at[longest] + 1) % extent[longest]
    return entries.at[tuple(index_at)].set(largest)


def shard_levels(stream_key, extent, cuts, least, high):
    def one(axis_at, blocks):
        steps = jax.random.uniform(jax.random.fold_in(jax.random.fold_in(stream_key, 6), axis_at), (blocks,), jnp.float32, least / len(cuts), high / len(cuts))
        return jnp.repeat(jnp.exp(steps), extent[axis_at] // blocks).reshape((-1,) + (1,) * (len(extent) - axis_at - 1))

    factor_of = one(*cuts[0])
    for cut in cuts[1:]:
        factor_of = factor_of * one(*cut)
    return factor_of


def centred(stream_key, shape, spread, reach, pieces=(), held_as=jnp.bfloat16):
    drawn = jax.random.normal(stream_key, shape, jnp.float32) * spread
    if len(pieces) > 0:
        drawn = shard_levels(stream_key, shape, pieces, -0.22, 0.18) * drawn
    return jnp.clip(drawn, min=-reach, max=reach).astype(held_as)


def setup_inputs(seed: int = 0) -> dict:
    key_of = jax.random.split(jax.random.key(seed), 6)
    latents = centred(key_of[0], (WINS, WF, P_SIZE, D), 1.0, 6.0, ((0, 32), (2, 16)))
    prompt_ids = touch_ends(jax.random.randint(key_of[1], (WINS,), 0, PROMPTS), jax.random.fold_in(key_of[1], 1), 0, PROMPTS - 1).astype(jnp.int32)
    modulation = draw_modulation(jax.random.fold_in(key_of[5], 71), 0)
    w_qkv = centred(key_of[3], (3, HEADS * HEAD_DIM, D), (2.0 * D ** -0.5), 0.5, ((1, 16),))
    intersection = draw_intersection(jax.random.fold_in(key_of[5], 71), 0)
    return {"latents": latents, "prompt_ids": prompt_ids, "modulation": modulation, "w_qkv": w_qkv, "intersection": intersection}


def selectors(ov_prev, ov_next, frames, most):
    fidx = jnp.arange(frames, dtype=jnp.int32)[:, None]
    jidx = jnp.arange(most, dtype=jnp.int32)[None, :]
    sel_prev = ((fidx < ov_prev) & (jidx == most - ov_prev + fidx)).astype(jnp.float32)
    sel_next = ((fidx >= frames - ov_next) & (jidx == fidx - frames + ov_next)).astype(jnp.float32)
    count = 1.0 + lax.optimization_barrier(jnp.sum(sel_prev, axis=1)) + lax.optimization_barrier(jnp.sum(sel_next, axis=1))
    return (sel_prev, sel_next, count)

def window_attention(latent, mods, w_qkv):
    xf = latent.astype(jnp.float32)
    mean = lax.optimization_barrier(jnp.mean(xf, axis=-1, keepdims=True))
    var = lax.optimization_barrier(jnp.mean((xf - mean) ** 2, axis=-1, keepdims=True))
    normed = ((xf - mean) / jnp.sqrt(var + 1e-06) * (1.0 + mods[1]) + mods[0]).astype(jnp.bfloat16)
    length = WF * P_SIZE
    qkv = lax.dot_general(normed.reshape(length, D), w_qkv.reshape(3 * D, D), (((1,), (1,)), ((), ())), preferred_element_type=jnp.float32)
    qkv = qkv.astype(jnp.bfloat16).reshape(length, 3, HEADS, HEAD_DIM)
    queries = jnp.transpose(qkv[:, 0], (1, 0, 2))
    keys = jnp.transpose(qkv[:, 1], (1, 0, 2))
    values = jnp.transpose(qkv[:, 2], (1, 0, 2))
    factor = HEAD_DIM ** (-0.5)

    def one_head(args):
        qh, kh, vh = args
        scores = jnp.dot(qh, kh.T, preferred_element_type=jnp.float32) * factor
        scores = scores - lax.optimization_barrier(jnp.max(scores, axis=-1, keepdims=True))
        expo = jnp.exp(scores)
        probs = (expo / lax.optimization_barrier(jnp.sum(expo, axis=-1, keepdims=True))).astype(jnp.bfloat16)
        return jnp.dot(probs, vh, preferred_element_type=jnp.float32).astype(jnp.bfloat16)
    heads_out = lax.map(one_head, (queries, keys, values))
    return jnp.transpose(heads_out, (1, 0, 2)).reshape(WF, P_SIZE, D)

def reference(latents, prompt_ids, modulation, w_qkv, intersection):
    mods = modulation[prompt_ids]
    attended = lax.map(lambda t: window_attention(t[0], t[1], w_qkv), (latents, mods))
    zeros = jnp.zeros((1, OMAX, P_SIZE, D), jnp.bfloat16)
    prev_tail = jnp.concatenate([zeros, attended[:-1, WF - OMAX:]], axis=0)
    next_head = jnp.concatenate([attended[1:, :OMAX], zeros], axis=0)
    ov_next = jnp.concatenate([intersection[1:], jnp.zeros((1,), jnp.int32)]).astype(jnp.int32)

    def blend(cur, prev, nxt, ov_p, ov_n):
        sel_prev, sel_next, count = selectors(ov_p, ov_n, WF, OMAX)
        total = cur.astype(jnp.float32)
        total = total + jnp.einsum('fj,jpe->fpe', sel_prev, prev.astype(jnp.float32), precision=lax.Precision.HIGHEST)
        total = total + jnp.einsum('fj,jpe->fpe', sel_next, nxt.astype(jnp.float32), precision=lax.Precision.HIGHEST)
        return (total / count[:, None, None]).astype(jnp.bfloat16)
    averaged = jax.vmap(blend)(attended, prev_tail, next_head, intersection, ov_next)
    gate = mods[:, 2][:, None, None, :]
    return (latents.astype(jnp.float32) + gate * averaged.astype(jnp.float32)).astype(jnp.bfloat16)
```

```python
import functools

import jax
import jax.numpy as jnp
from jax import lax
from jax.experimental import pallas as pl
from jax.experimental.pallas import tpu as pltpu
from jax.sharding import Mesh
from jax.sharding import PartitionSpec as P

HEAD_DIM = 64
OMAX = 3
NX, NY, NC = 4, 2, 2
MIB = 1 << 20
OFFSETS = (0, 3, 1, 2)


def project_kernel(pid, t0, t1, t2, t3, mod_ref, wa, wb, oa, ob, va, vb, sems):
    copies = [pltpu.make_async_copy(wa, va, sems.at[0]), pltpu.make_async_copy(wb, vb, sems.at[1])]
    for c in copies:
        c.start()
    shift = mod_ref[0, 0:1, :]
    scale = 1.0 + mod_ref[0, 1:2, :]
    parts = []
    for t in (t0, t1, t2, t3):
        xf = t[...].astype(jnp.float32)
        mean = jnp.mean(xf, axis=-1, keepdims=True)
        xc = xf - mean
        var = jnp.mean(xc * xc, axis=-1, keepdims=True)
        parts.append((xc * lax.rsqrt(var + 1e-06) * scale + shift).astype(jnp.bfloat16))
    normed = jnp.concatenate(parts, axis=0)
    for c, v, o in zip(copies, (va, vb), (oa, ob)):
        c.wait()
        o[...] = lax.dot_general(
            normed, v[...], (((1,), (1,)), ((), ())), preferred_element_type=jnp.float32
        ).astype(jnp.bfloat16)


def project(pid, blocks, modulation, wa, wb):
    rows, width = blocks[0].shape
    feats = wa.shape[0]
    tok = pl.BlockSpec((rows, width), lambda i, p: (0, 0))
    out = pl.BlockSpec((4 * rows, feats), lambda i, p: (0, 0))
    hbm = pl.BlockSpec(memory_space=pl.ANY)
    shape = jax.ShapeDtypeStruct((4 * rows, feats), jnp.bfloat16)
    return pl.pallas_call(
        project_kernel,
        grid_spec=pltpu.PrefetchScalarGridSpec(
            num_scalar_prefetch=1,
            grid=(1,),
            in_specs=[tok] * 4 + [pl.BlockSpec((1, 3, width), lambda i, p: (p[0], 0, 0)), hbm, hbm],
            out_specs=[out, out],
            scratch_shapes=[
                pltpu.VMEM((feats, width), jnp.bfloat16),
                pltpu.VMEM((feats, width), jnp.bfloat16),
                pltpu.SemaphoreType.DMA((2,)),
            ],
        ),
        out_shape=[shape, shape],
        compiler_params=pltpu.CompilerParams(vmem_limit_bytes=48 * MIB),
    )(pid, *blocks, modulation, wa, wb)


def attend_kernel(first, count, place, g0, g1, g2, g3, out):
    groups = (g0, g1, g2, g3)
    per = g0.shape[0]
    rows = g0.shape[1]
    width = g0.shape[2] // 3
    keys = per * rows
    lane = lax.broadcasted_iota(jnp.int32, (4 * keys, 128), 1)
    heads = width // HEAD_DIM
    kk, vv = [], []
    for h in range(heads):
        a = width + h * HEAD_DIM
        kk.append(jnp.concatenate([g[:, :, a : a + HEAD_DIM].reshape(keys, HEAD_DIM) for g in groups], axis=0))
        a = 2 * width + h * HEAD_DIM
        v = jnp.concatenate([g[:, :, a : a + HEAD_DIM].reshape(keys, HEAD_DIM) for g in groups], axis=0)
        v = jnp.concatenate([v, jnp.zeros_like(v)], axis=1)
        vv.append(jnp.where(lane == HEAD_DIM, jnp.ones_like(v), v))
    for pair in (0, 2):
        results = []
        for h in range(heads):
            a = h * HEAD_DIM
            q = jnp.concatenate(
                [
                    g[:, first : first + count, a : a + HEAD_DIM].reshape(per * count, HEAD_DIM)
                    for g in groups[pair : pair + 2]
                ],
                axis=0,
            )
            s = lax.dot_general(q, kk[h], (((1,), (1,)), ((), ())), preferred_element_type=jnp.float32)
            top = jnp.max(s, axis=-1, keepdims=True)
            p = jnp.exp((s - top) * (HEAD_DIM**-0.5)).astype(jnp.bfloat16)
            o = lax.dot_general(p, vv[h], (((1,), (0,)), ((), ())), preferred_element_type=jnp.float32)
            results.append(o[:, :HEAD_DIM] / o[:, HEAD_DIM : HEAD_DIM + 1])
        both = jnp.concatenate(results, axis=1).astype(jnp.bfloat16).reshape(2 * per, count, width)
        for j in range(2):
            group = pair + j
            for n in range(per):
                x = lax.rem(place[0] + OFFSETS[n], NX)
                y = lax.rem(place[1] + group // 2, NY)
                c = lax.rem(place[2] + group % 2, NC)
                out[(x * NY + y) * NC + c] = both[j * per + n]


def attend(first, count, place, groups):
    per, rows, feats = groups[0].shape
    full = pl.BlockSpec(memory_space=pltpu.VMEM)
    return pl.pallas_call(
        functools.partial(attend_kernel, first, count),
        in_specs=[pl.BlockSpec(memory_space=pltpu.SMEM)] + [full] * 4,
        out_specs=full,
        out_shape=jax.ShapeDtypeStruct((4 * per, count, feats // 3), jnp.bfloat16),
        compiler_params=pltpu.CompilerParams(vmem_limit_bytes=48 * MIB),
    )(place, *groups)


def average_kernel(overlap, low, high, before, after, out):
    half = low.shape[1]
    each = 8
    frames = 2 * half // each
    ov_prev, ov_next = overlap[0], overlap[1]
    prev = before[...].astype(jnp.float32)
    nxt = after[...].astype(jnp.float32)
    for ref, base in ((low, 0), (high, frames // 2)):
        mine = ref[...].astype(jnp.float32)
        done = []
        for i in range(frames // 2):
            f = base + i
            cur = mine[:, i * each : (i + 1) * each]
            if f < OMAX:
                shared = f < ov_prev
                part = jnp.zeros_like(cur)
                for j in range(OMAX):
                    at = (frames // 2 - OMAX + j) * each
                    take = shared & (j == OMAX - ov_prev + f)
                    part = jnp.where(take, prev[:, at : at + each], part)
                cur = (cur + part) * jnp.where(shared, 0.5, 1.0)
            if f >= frames - OMAX:
                shared = f >= frames - ov_next
                part = jnp.zeros_like(cur)
                for j in range(OMAX):
                    take = shared & (j == f - frames + ov_next)
                    part = jnp.where(take, nxt[:, j * each : (j + 1) * each], part)
                cur = (cur + part) * jnp.where(shared, 0.5, 1.0)
            done.append(cur)
        out[:, base * each : base * each + half, :] = jnp.concatenate(done, axis=1).astype(jnp.bfloat16)


def average(overlap, low, high, before, after):
    full = pl.BlockSpec(memory_space=pltpu.VMEM)
    blocks, half, width = low.shape
    return pl.pallas_call(
        average_kernel,
        in_specs=[pl.BlockSpec(memory_space=pltpu.SMEM)] + [full] * 4,
        out_specs=full,
        out_shape=jax.ShapeDtypeStruct((blocks, 2 * half, width), jnp.bfloat16),
        compiler_params=pltpu.CompilerParams(vmem_limit_bytes=32 * MIB),
    )(overlap, low, high, before, after)


def blend_kernel(pid, lat, mod_ref, avg, out):
    blocks, _, width = avg.shape
    for b in range(0, blocks, 2):
        cols = slice(b * width, (b + 2) * width)
        a = jnp.concatenate([avg[b].astype(jnp.float32), avg[b + 1].astype(jnp.float32)], axis=1)
        out[:, cols] = (lat[:, cols].astype(jnp.float32) + mod_ref[0, 2:3, cols] * a).astype(jnp.bfloat16)


def blend(pid, lat, modulation, avg):
    rows, width = lat.shape
    tok = pl.BlockSpec((rows, width), lambda i, p: (0, 0))
    return pl.pallas_call(
        blend_kernel,
        grid_spec=pltpu.PrefetchScalarGridSpec(
            num_scalar_prefetch=1,
            grid=(1,),
            in_specs=[
                tok,
                pl.BlockSpec((1, 3, width), lambda i, p: (p[0], 0, 0)),
                pl.BlockSpec(avg.shape, lambda i, p: (0, 0, 0)),
            ],
            out_specs=tok,
        ),
        out_shape=jax.ShapeDtypeStruct((rows, width), jnp.bfloat16),
        compiler_params=pltpu.CompilerParams(vmem_limit_bytes=32 * MIB),
    )(pid, lat, modulation, avg)


def around(value, axis, by):
    n = lax.axis_size(axis)
    return lax.ppermute(value, axis, [(i, (i + by) % n) for i in range(n)])


def along(value, by):
    n = lax.axis_size(("ylo", "z"))
    return lax.ppermute(value, ("ylo", "z"), [(i, i + by) for i in range(n) if 0 <= i + by < n])


def shards(latents, prompt_ids, modulation, w_qkv, intersection):
    _, frames, patches, width = latents.shape
    rows = frames * patches
    mine = latents.reshape(rows, width)
    wa = w_qkv.reshape(-1, width)
    place = jnp.stack([lax.axis_index("x"), lax.axis_index("yhi"), lax.axis_index("core")]).astype(jnp.int32)

    other = around(mine, "yhi", 1)
    near = [mine] + [around(mine, "x", by) for by in (1, 3, 2)]
    wb = around(wa, "core", 1)
    far = [other] + [around(other, "x", by) for by in (1, 3, 2)]

    own0, give0 = project(prompt_ids, near, modulation, wa, wb)
    got0 = around(give0, "core", 1)
    own1, give1 = project(prompt_ids, far, modulation, wa, wb)
    got1 = around(give1, "core", 1)
    groups = [g.reshape(4, rows, -1) for g in (own0, got0, own1, got1)]

    low = attend(0, rows // 2, place, groups)
    after = along(low, -1)
    high = attend(rows // 2, rows // 2, place, groups)
    before = along(high, 1)

    window = lax.axis_index(("ylo", "z"))
    padded = jnp.concatenate([intersection, jnp.zeros((1,), jnp.int32)])
    overlap = lax.dynamic_slice(padded, (window,), (2,))
    avg = average(overlap, low, high, before, after)
    avg = lax.all_to_all(avg, ("x", "yhi", "core"), 0, 0)
    return blend(prompt_ids, mine, modulation, avg).reshape(latents.shape)


def solution(mesh):
    fine = Mesh(mesh.devices.reshape(4, 8, NX, NY, NC), ("ylo", "z", "x", "yhi", "core"))
    win, head = ("ylo", "z"), ("x", "yhi", "core")
    in_specs = (P(win, None, head, None), P(win), P(), P(None, head, None), P())
    out_specs = P(win, None, head, None)
    return jax.shard_map(shards, mesh=fine, in_specs=in_specs, out_specs=out_specs, check_vma=False)
```

```python
import functools

import jax
import jax.numpy as jnp
from jax import lax
from jax.experimental import pallas as pl
from jax.experimental.pallas import tpu as pltpu
from jax.sharding import Mesh
from jax.sharding import PartitionSpec as P

HEAD_DIM = 64
OMAX = 3
NX, NY, NC = 4, 2, 2
MIB = 1 << 20
OFFSETS = (0, 3, 1, 2)


def cost(flops, inputs, outputs, transcendentals=0):
    size = sum(a.size * a.dtype.itemsize for a in (*inputs, *outputs))
    return pl.CostEstimate(flops=flops, bytes_accessed=size, transcendentals=transcendentals)


def project_kernel(pid, t0, t1, t2, t3, mod_ref, wa, wb, oa, ob):
    row = pl.ds(pid[0], 1)
    shift = mod_ref[0, row, :]
    scale = 1.0 + mod_ref[1, row, :]
    parts = []
    for t in (t0, t1, t2, t3):
        xf = t[...].astype(jnp.float32)
        mean = jnp.mean(xf, axis=-1, keepdims=True)
        xc = xf - mean
        var = jnp.mean(xc * xc, axis=-1, keepdims=True)
        parts.append((xc * lax.rsqrt(var + 1e-06) * scale + shift).astype(jnp.bfloat16))
    normed = jnp.concatenate(parts, axis=0)
    for w, o in ((wa, oa), (wb, ob)):
        o[...] = lax.dot_general(
            normed, w[...], (((1,), (1,)), ((), ())), preferred_element_type=jnp.float32
        ).astype(jnp.bfloat16)


def project(pid, blocks, modulation, wa, wb):
    rows, width = blocks[0].shape
    feats = wa.shape[0]
    full = pl.BlockSpec(memory_space=pltpu.VMEM)
    shape = jax.ShapeDtypeStruct((4 * rows, feats), jnp.bfloat16)
    return pl.pallas_call(
        project_kernel,
        in_specs=[pl.BlockSpec(memory_space=pltpu.SMEM)] + [full] * 7,
        out_specs=[full, full],
        out_shape=[shape, shape],
        cost_estimate=cost(16 * rows * feats * width, (*blocks, wa, wb), (shape, shape)),
        compiler_params=pltpu.CompilerParams(vmem_limit_bytes=24 * MIB),
    )(pid, *blocks, modulation, wa, wb)


def attend_kernel(first, count, place, g0, g1, g2, g3, out):
    groups = (g0, g1, g2, g3)
    per = g0.shape[0]
    rows = g0.shape[1]
    width = g0.shape[2] // 3
    keys = per * rows
    lane = lax.broadcasted_iota(jnp.int32, (4 * keys, 128), 1)
    heads = width // HEAD_DIM
    kk, vv = [], []
    for h in range(heads):
        a = width + h * HEAD_DIM
        kk.append(jnp.concatenate([g[:, :, a : a + HEAD_DIM].reshape(keys, HEAD_DIM) for g in groups], axis=0))
        a = 2 * width + h * HEAD_DIM
        v = jnp.concatenate([g[:, :, a : a + HEAD_DIM].reshape(keys, HEAD_DIM) for g in groups], axis=0)
        v = jnp.concatenate([v, jnp.zeros_like(v)], axis=1)
        vv.append(jnp.where(lane == HEAD_DIM, jnp.ones_like(v), v))
    for pair in (0, 2):
        results = []
        for h in range(heads):
            a = h * HEAD_DIM
            q = jnp.concatenate(
                [
                    g[:, first : first + count, a : a + HEAD_DIM].reshape(per * count, HEAD_DIM)
                    for g in groups[pair : pair + 2]
                ],
                axis=0,
            )
            s = lax.dot_general(q, kk[h], (((1,), (1,)), ((), ())), preferred_element_type=jnp.float32)
            top = jnp.max(s, axis=-1, keepdims=True)
            p = jnp.exp((s - top) * (HEAD_DIM**-0.5)).astype(jnp.bfloat16)
            o = lax.dot_general(p, vv[h], (((1,), (0,)), ((), ())), preferred_element_type=jnp.float32)
            results.append(o[:, :HEAD_DIM] / o[:, HEAD_DIM : HEAD_DIM + 1])
        both = jnp.concatenate(results, axis=1).astype(jnp.bfloat16).reshape(2 * per, count, width)
        for j in range(2):
            group = pair + j
            for n in range(per):
                x = lax.rem(place[0] + OFFSETS[n], NX)
                y = lax.rem(place[1] + group // 2, NY)
                c = lax.rem(place[2] + group % 2, NC)
                out[(x * NY + y) * NC + c] = both[j * per + n]


def attend(first, count, place, groups):
    per, rows, feats = groups[0].shape
    full = pl.BlockSpec(memory_space=pltpu.VMEM)
    shape = jax.ShapeDtypeStruct((4 * per, count, feats // 3), jnp.bfloat16)
    scores = 16 * per * per * count * rows * (feats // 3 // HEAD_DIM)
    return pl.pallas_call(
        functools.partial(attend_kernel, first, count),
        in_specs=[pl.BlockSpec(memory_space=pltpu.SMEM)] + [full] * 4,
        out_specs=full,
        out_shape=shape,
        cost_estimate=cost(16 * HEAD_DIM * scores, groups, (shape,), scores),
        compiler_params=pltpu.CompilerParams(vmem_limit_bytes=24 * MIB),
    )(place, *groups)


def average_kernel(overlap, low, high, before, after, out):
    half = low.shape[1]
    each = 8
    frames = 2 * half // each
    ov_prev, ov_next = overlap[0], overlap[1]
    prev = before[...].astype(jnp.float32)
    nxt = after[...].astype(jnp.float32)
    for ref, base in ((low, 0), (high, frames // 2)):
        mine = ref[...].astype(jnp.float32)
        done = []
        for i in range(frames // 2):
            f = base + i
            cur = mine[:, i * each : (i + 1) * each]
            if f < OMAX:
                shared = f < ov_prev
                part = jnp.zeros_like(cur)
                for j in range(OMAX):
                    at = (frames // 2 - OMAX + j) * each
                    take = shared & (j == OMAX - ov_prev + f)
                    part = jnp.where(take, prev[:, at : at + each], part)
                cur = (cur + part) * jnp.where(shared, 0.5, 1.0)
            if f >= frames - OMAX:
                shared = f >= frames - ov_next
                part = jnp.zeros_like(cur)
                for j in range(OMAX):
                    take = shared & (j == f - frames + ov_next)
                    part = jnp.where(take, nxt[:, j * each : (j + 1) * each], part)
                cur = (cur + part) * jnp.where(shared, 0.5, 1.0)
            done.append(cur)
        out[:, base * each : base * each + half, :] = jnp.concatenate(done, axis=1).astype(jnp.bfloat16)


def average(overlap, low, high, before, after):
    full = pl.BlockSpec(memory_space=pltpu.VMEM)
    blocks, half, width = low.shape
    return pl.pallas_call(
        average_kernel,
        in_specs=[pl.BlockSpec(memory_space=pltpu.SMEM)] + [full] * 4,
        out_specs=full,
        out_shape=jax.ShapeDtypeStruct((blocks, 2 * half, width), jnp.bfloat16),
        compiler_params=pltpu.CompilerParams(vmem_limit_bytes=16 * MIB),
    )(overlap, low, high, before, after)


def blend_kernel(pid, lat, mod_ref, avg, out):
    blocks, _, width = avg.shape
    gate = mod_ref[2, pl.ds(pid[0], 1), :]
    for b in range(0, blocks, 2):
        cols = slice(b * width, (b + 2) * width)
        a = jnp.concatenate([avg[b].astype(jnp.float32), avg[b + 1].astype(jnp.float32)], axis=1)
        out[:, cols] = (lat[:, cols].astype(jnp.float32) + gate[:, cols] * a).astype(jnp.bfloat16)


def blend(pid, lat, modulation, avg):
    full = pl.BlockSpec(memory_space=pltpu.VMEM)
    return pl.pallas_call(
        blend_kernel,
        in_specs=[pl.BlockSpec(memory_space=pltpu.SMEM)] + [full] * 3,
        out_specs=full,
        out_shape=jax.ShapeDtypeStruct(lat.shape, jnp.bfloat16),
        compiler_params=pltpu.CompilerParams(vmem_limit_bytes=16 * MIB),
    )(pid, lat, modulation, avg)


def around(value, axis, by):
    n = lax.axis_size(axis)
    return lax.ppermute(value, axis, [(i, (i + by) % n) for i in range(n)])


def along(value, by):
    n = lax.axis_size(("ylo", "z"))
    return lax.ppermute(value, ("ylo", "z"), [(i, i + by) for i in range(n) if 0 <= i + by < n])


def shards(latents, prompt_ids, modulation, w_qkv, intersection):
    _, frames, patches, width = latents.shape
    rows = frames * patches
    mine = latents.reshape(rows, width)
    wa = w_qkv.reshape(-1, width)
    place = jnp.stack([lax.axis_index("x"), lax.axis_index("yhi"), lax.axis_index("core")]).astype(jnp.int32)

    modulation = jnp.transpose(modulation, (1, 0, 2))
    other = around(mine, "yhi", 1)
    near = [mine] + [around(mine, "x", by) for by in (1, 3, 2)]
    wb = around(wa, "core", 1)
    other, *near = lax.optimization_barrier((other, *near))
    far = [other] + [around(other, "x", by) for by in (1, 3, 2)]

    own0, give0 = project(prompt_ids, near, modulation, wa, wb)
    got0 = around(give0, "core", 1)
    own1, give1 = project(prompt_ids, far, modulation, wa, wb)
    got1 = around(give1, "core", 1)
    groups = [g.reshape(4, rows, -1) for g in (own0, got0, own1, got1)]

    low = attend(0, rows // 2, place, groups)
    after = along(low, -1)
    high = attend(rows // 2, rows // 2, place, groups)
    before = along(high, 1)

    window = lax.axis_index(("ylo", "z"))
    padded = jnp.concatenate([intersection, jnp.zeros((1,), jnp.int32)])
    overlap = lax.dynamic_slice(padded, (window,), (2,))
    avg = average(overlap, low, high, before, after)
    avg = lax.all_to_all(avg, ("x", "yhi", "core"), 0, 0)
    return blend(prompt_ids, mine, modulation, avg).reshape(latents.shape)


def solution(mesh):
    fine = Mesh(mesh.devices.reshape(4, 8, NX, NY, NC), ("ylo", "z", "x", "yhi", "core"))
    win, head = ("ylo", "z"), ("x", "yhi", "core")
    in_specs = (P(win, None, head, None), P(win), P(), P(None, head, None), P())
    out_specs = P(win, None, head, None)
    return jax.shard_map(shards, mesh=fine, in_specs=in_specs, out_specs=out_specs, check_vma=False)
```

```python
import functools

import jax
import jax.numpy as jnp
from jax import lax
from jax.experimental import pallas as pl
from jax.experimental.pallas import tpu as pltpu
from jax.sharding import Mesh
from jax.sharding import PartitionSpec as P

HEAD_DIM = 64
OMAX = 3
NX, NY, NC = 4, 2, 2
MIB = 1 << 20
OFFSETS = (0, 3, 1, 2)


def cost(flops, inputs, outputs, transcendentals=0):
    size = sum(a.size * a.dtype.itemsize for a in (*inputs, *outputs))
    return pl.CostEstimate(flops=flops, bytes_accessed=size, transcendentals=transcendentals)


def project_kernel(blocks, pid, *refs):
    tokens, mod_ref, rest = refs[:blocks], refs[blocks], refs[blocks + 1 :]
    row = pl.ds(pid[0], 1)
    shift = mod_ref[0, row, :]
    scale = 1.0 + mod_ref[1, row, :]
    parts = []
    for t in tokens:
        for i in range(0, t.shape[0], 64):
            xf = t[i : i + 64].astype(jnp.float32)
            mean = jnp.mean(xf, axis=-1, keepdims=True)
            xc = xf - mean
            var = jnp.mean(xc * xc, axis=-1, keepdims=True)
            parts.append((xc * lax.rsqrt(var + 1e-06) * scale + shift).astype(jnp.bfloat16))
    normed = jnp.concatenate(parts, axis=0)
    half = len(rest) // 2
    for w, o in zip(rest[:half], rest[half:]):
        o[...] = lax.dot_general(
            normed, w[...], (((1,), (1,)), ((), ())), preferred_element_type=jnp.float32
        ).astype(jnp.bfloat16)


def project(pid, blocks, modulation, weights):
    rows = sum(b.shape[0] for b in blocks)
    feats, width = weights[0].shape
    full = pl.BlockSpec(memory_space=pltpu.VMEM)
    shapes = [jax.ShapeDtypeStruct((rows, feats), jnp.bfloat16)] * len(weights)
    return pl.pallas_call(
        functools.partial(project_kernel, len(blocks)),
        in_specs=[pl.BlockSpec(memory_space=pltpu.SMEM)] + [full] * (len(blocks) + 1 + len(weights)),
        out_specs=[full] * len(weights),
        out_shape=shapes,
        cost_estimate=cost(2 * rows * feats * width * len(weights), (*blocks, *weights), shapes),
        compiler_params=pltpu.CompilerParams(vmem_limit_bytes=24 * MIB),
    )(pid, *blocks, modulation, *weights)


def attend_kernel(first, count, place, near, far, swapped, out):
    groups = (near, far, swapped)
    width = near.shape[2] // 3
    heads = width // HEAD_DIM

    def columns(refs, part, h, rows=slice(None)):
        a = part * width + h * HEAD_DIM
        taken = [g[:, rows, a : a + HEAD_DIM] for g in refs]
        return jnp.concatenate([t.reshape(-1, HEAD_DIM) for t in taken], axis=0)

    kk, vv = [], []
    for h in range(heads):
        kk.append(columns(groups, 1, h))
        v = columns(groups, 2, h)
        lane = lax.broadcasted_iota(jnp.int32, (v.shape[0], 2 * HEAD_DIM), 1)
        vv.append(jnp.where(lane == HEAD_DIM, jnp.ones_like(v[:1, :1]), jnp.concatenate([v, jnp.zeros_like(v)], axis=1)))
    for refs in ((near,), (far, swapped)):
        results = []
        for h in range(heads):
            q = columns(refs, 0, h, slice(first, first + count))
            s = lax.dot_general(q, kk[h], (((1,), (1,)), ((), ())), preferred_element_type=jnp.float32)
            top = jnp.max(s, axis=-1, keepdims=True)
            p = jnp.exp((s - top) * (HEAD_DIM**-0.5)).astype(jnp.bfloat16)
            o = lax.dot_general(p, vv[h], (((1,), (0,)), ((), ())), preferred_element_type=jnp.float32)
            results.append(o[:, :HEAD_DIM] / o[:, HEAD_DIM : HEAD_DIM + 1])
        both = jnp.concatenate(results, axis=1).astype(jnp.bfloat16).reshape(-1, count, width)
        for n in range(both.shape[0]):
            if refs[0] is near:
                x, y, c = n // NC, place[1], n % NC
            else:
                x = lax.rem(place[0] + OFFSETS[n % NX], NX)
                y = 1 - place[1]
                c = place[2] if n < NX else 1 - place[2]
            out[(x * NY + y) * NC + c] = both[n]


def attend(first, count, place, groups):
    blocks = sum(g.shape[0] for g in groups)
    _, rows, feats = groups[0].shape
    full = pl.BlockSpec(memory_space=pltpu.VMEM)
    shape = jax.ShapeDtypeStruct((blocks, count, feats // 3), jnp.bfloat16)
    scores = blocks * blocks * count * rows * (feats // 3 // HEAD_DIM)
    return pl.pallas_call(
        functools.partial(attend_kernel, first, count),
        in_specs=[pl.BlockSpec(memory_space=pltpu.SMEM)] + [full] * 3,
        out_specs=full,
        out_shape=shape,
        cost_estimate=cost(4 * HEAD_DIM * scores, groups, (shape,), scores),
        compiler_params=pltpu.CompilerParams(vmem_limit_bytes=24 * MIB),
    )(place, *groups)


def join(mine, shared, takes):
    part = jnp.zeros_like(mine)
    for take, other in takes:
        part = jnp.where(take, other, part)
    return (mine + part) * jnp.where(shared, 0.5, 1.0)


def average_high_kernel(overlap, high, after, out):
    half = high.shape[1]
    each = 8
    count = half // each
    ov_next = overlap[1]
    mine = high[...].astype(jnp.float32)
    nxt = after[...].astype(jnp.float32)
    done = []
    for i in range(count):
        cur = mine[:, i * each : (i + 1) * each]
        if i >= count - OMAX:
            takes = [(j == i - count + ov_next, nxt[:, j * each : (j + 1) * each]) for j in range(OMAX)]
            cur = join(cur, i >= count - ov_next, takes)
        done.append(cur)
    out[...] = jnp.concatenate(done, axis=1).astype(jnp.bfloat16)


def average_low_kernel(overlap, low, before, high, out):
    half = low.shape[1]
    each = 8
    count = half // each
    ov_prev = overlap[0]
    mine = low[...].astype(jnp.float32)
    prev = before[...].astype(jnp.float32)
    done = []
    for i in range(count):
        cur = mine[:, i * each : (i + 1) * each]
        if i < OMAX:
            takes = [
                (j == OMAX - ov_prev + i, prev[:, (count - OMAX + j) * each : (count - OMAX + j + 1) * each])
                for j in range(OMAX)
            ]
            cur = join(cur, i < ov_prev, [((i < ov_prev) & t, o) for t, o in takes])
        done.append(cur)
    out[:, :half, :] = jnp.concatenate(done, axis=1).astype(jnp.bfloat16)
    out[:, half:, :] = high[...]


def average(kernel, overlap, parts, rows):
    full = pl.BlockSpec(memory_space=pltpu.VMEM)
    blocks, _, width = parts[0].shape
    shape = jax.ShapeDtypeStruct((blocks, rows, width), jnp.bfloat16)
    return pl.pallas_call(
        kernel,
        in_specs=[pl.BlockSpec(memory_space=pltpu.SMEM)] + [full] * len(parts),
        out_specs=full,
        out_shape=shape,
        cost_estimate=cost(8 * blocks * rows * width, parts, (shape,)),
        compiler_params=pltpu.CompilerParams(vmem_limit_bytes=16 * MIB),
    )(overlap, *parts)


def blend_kernel(pid, lat, mod_ref, avg, out):
    blocks, _, width = avg.shape
    gate = mod_ref[2, pl.ds(pid[0], 1), :]
    for b in range(0, blocks, 2):
        cols = slice(b * width, (b + 2) * width)
        a = jnp.concatenate([avg[b].astype(jnp.float32), avg[b + 1].astype(jnp.float32)], axis=1)
        out[:, cols] = (lat[:, cols].astype(jnp.float32) + gate[:, cols] * a).astype(jnp.bfloat16)


def blend(pid, lat, modulation, avg):
    full = pl.BlockSpec(memory_space=pltpu.VMEM)
    return pl.pallas_call(
        blend_kernel,
        in_specs=[pl.BlockSpec(memory_space=pltpu.SMEM)] + [full] * 3,
        out_specs=full,
        out_shape=jax.ShapeDtypeStruct(lat.shape, jnp.bfloat16),
        compiler_params=pltpu.CompilerParams(vmem_limit_bytes=16 * MIB),
    )(pid, lat, modulation, avg)


def around(value, axis, by):
    n = lax.axis_size(axis)
    return lax.ppermute(value, axis, [(i, (i + by) % n) for i in range(n)])


def along(value, by):
    n = lax.axis_size(("ylo", "z"))
    return lax.ppermute(value, ("ylo", "z"), [(i, i + by) for i in range(n) if 0 <= i + by < n])


def shards(latents, prompt_ids, modulation, w_qkv, intersection):
    _, frames, patches, width = latents.shape
    rows = frames * patches
    mine = latents.reshape(rows, width)
    wa = w_qkv.reshape(-1, width)
    place = jnp.stack([lax.axis_index("x"), lax.axis_index("yhi"), lax.axis_index("core")]).astype(jnp.int32)

    modulation = jnp.transpose(modulation, (1, 0, 2))
    window = lax.axis_index(("ylo", "z"))
    padded = jnp.concatenate([intersection, jnp.zeros((1,), jnp.int32)])
    overlap = lax.dynamic_slice(padded, (window,), (2,))

    near = lax.all_gather(mine, ("x", "core"), axis=0, tiled=True)
    other = around(mine, "yhi", 1)
    wb = around(wa, "core", 1)
    far = [other] + [around(other, "x", by) for by in (1, 3, 2)]

    own, give = project(prompt_ids, far, modulation, [wa, wb])
    got = around(give, "core", 1)
    (home,) = project(prompt_ids, [near], modulation, [wa])
    groups = [g.reshape(-1, rows, g.shape[-1]) for g in (home, own, got)]

    half = rows // 2
    low = attend(0, half, place, groups)
    after = along(low, -1)
    high = attend(half, half, place, groups)
    before = along(high, 1)

    avg = average(average_high_kernel, overlap, (high, after), half)
    avg = average(average_low_kernel, overlap, (low, before, avg), rows)
    avg = lax.all_to_all(avg, ("x", "yhi", "core"), 0, 0)
    return blend(prompt_ids, mine, modulation, avg).reshape(latents.shape)


def solution(mesh):
    fine = Mesh(mesh.devices.reshape(4, 8, NX, NY, NC), ("ylo", "z", "x", "yhi", "core"))
    win, head = ("ylo", "z"), ("x", "yhi", "core")
    in_specs = (P(win, None, head, None), P(win), P(), P(None, head, None), P())
    out_specs = P(win, None, head, None)
    return jax.shard_map(shards, mesh=fine, in_specs=in_specs, out_specs=out_specs, check_vma=False)
```

```python
import functools

import jax
import jax.numpy as jnp
from jax import lax
from jax.experimental import pallas as pl
from jax.experimental.pallas import tpu as pltpu
from jax.sharding import Mesh
from jax.sharding import PartitionSpec as P

HEAD_DIM = 64
OMAX = 3
NX, NY, NC = 4, 2, 2
MIB = 1 << 20
OFFSETS = (0, 3, 1, 2)


def cost(flops, inputs, outputs, transcendentals=0):
    size = sum(a.size * a.dtype.itemsize for a in (*inputs, *outputs))
    return pl.CostEstimate(flops=flops, bytes_accessed=size, transcendentals=transcendentals)


def project_kernel(blocks, pid, *refs):
    tokens, mod_ref, rest = refs[:blocks], refs[blocks], refs[blocks + 1 :]
    row = pl.ds(pid[0], 1)
    shift = mod_ref[0, row, :]
    scale = 1.0 + mod_ref[1, row, :]
    parts = []
    for t in tokens:
        for i in range(0, t.shape[0], 64):
            xf = t[i : i + 64].astype(jnp.float32)
            mean = jnp.mean(xf, axis=-1, keepdims=True)
            xc = xf - mean
            var = jnp.mean(xc * xc, axis=-1, keepdims=True)
            parts.append((xc * lax.rsqrt(var + 1e-06) * scale + shift).astype(jnp.bfloat16))
    normed = jnp.concatenate(parts, axis=0)
    half = len(rest) // 2
    for w, o in zip(rest[:half], rest[half:]):
        o[...] = lax.dot_general(
            normed, w[...], (((1,), (1,)), ((), ())), preferred_element_type=jnp.float32
        ).astype(jnp.bfloat16)


def project(pid, blocks, modulation, weights):
    rows = sum(b.shape[0] for b in blocks)
    feats, width = weights[0].shape
    full = pl.BlockSpec(memory_space=pltpu.VMEM)
    shapes = [jax.ShapeDtypeStruct((rows, feats), jnp.bfloat16)] * len(weights)
    return pl.pallas_call(
        functools.partial(project_kernel, len(blocks)),
        in_specs=[pl.BlockSpec(memory_space=pltpu.SMEM)] + [full] * (len(blocks) + 1 + len(weights)),
        out_specs=[full] * len(weights),
        out_shape=shapes,
        cost_estimate=cost(2 * rows * feats * width * len(weights), (*blocks, *weights), shapes),
        compiler_params=pltpu.CompilerParams(vmem_limit_bytes=24 * MIB),
    )(pid, *blocks, modulation, *weights)


def attend_kernel(first, count, place, *refs):
    groups, out = refs[:-1], refs[-1]
    width = groups[0].shape[2] // 3
    heads = width // HEAD_DIM

    def columns(refs, part, h, rows=slice(None)):
        a = part * width + h * HEAD_DIM
        taken = [g[:, rows, a : a + HEAD_DIM] for g in refs]
        return jnp.concatenate([t.reshape(-1, HEAD_DIM) for t in taken], axis=0)

    kk, vv = [], []
    for h in range(heads):
        kk.append(columns(groups, 1, h))
        v = columns(groups, 2, h)
        lane = lax.broadcasted_iota(jnp.int32, (v.shape[0], 2 * HEAD_DIM), 1)
        vv.append(jnp.where(lane == HEAD_DIM, jnp.ones_like(v[:1, :1]), jnp.concatenate([v, jnp.zeros_like(v)], axis=1)))
    for pair in range(0, len(groups), 2):
        results = []
        for h in range(heads):
            q = columns(groups[pair : pair + 2], 0, h, slice(first, first + count))
            s = lax.dot_general(q, kk[h], (((1,), (1,)), ((), ())), preferred_element_type=jnp.float32)
            top = jnp.max(s, axis=-1, keepdims=True)
            p = jnp.exp((s - top) * (HEAD_DIM**-0.5)).astype(jnp.bfloat16)
            o = lax.dot_general(p, vv[h], (((1,), (0,)), ((), ())), preferred_element_type=jnp.float32)
            results.append(o[:, :HEAD_DIM] / o[:, HEAD_DIM : HEAD_DIM + 1])
        both = jnp.concatenate(results, axis=1).astype(jnp.bfloat16).reshape(-1, count, width)
        for n in range(both.shape[0]):
            x = lax.rem(place[0] + OFFSETS[n % NX], NX)
            y = place[1] if pair == 0 else 1 - place[1]
            c = place[2] if n < NX else 1 - place[2]
            out[(x * NY + y) * NC + c] = both[n]


def attend(first, count, place, groups):
    blocks = sum(g.shape[0] for g in groups)
    _, rows, feats = groups[0].shape
    full = pl.BlockSpec(memory_space=pltpu.VMEM)
    shape = jax.ShapeDtypeStruct((blocks, count, feats // 3), jnp.bfloat16)
    scores = blocks * blocks * count * rows * (feats // 3 // HEAD_DIM)
    return pl.pallas_call(
        functools.partial(attend_kernel, first, count),
        in_specs=[pl.BlockSpec(memory_space=pltpu.SMEM)] + [full] * len(groups),
        out_specs=full,
        out_shape=shape,
        cost_estimate=cost(4 * HEAD_DIM * scores, groups, (shape,), scores),
        compiler_params=pltpu.CompilerParams(vmem_limit_bytes=24 * MIB),
    )(place, *groups)


def join(mine, shared, takes):
    part = jnp.zeros_like(mine)
    for take, other in takes:
        part = jnp.where(take, other, part)
    return (mine + part) * jnp.where(shared, 0.5, 1.0)


def average_high_kernel(overlap, high, after, out):
    half = high.shape[1]
    each = 8
    count = half // each
    ov_next = overlap[1]
    mine = high[...].astype(jnp.float32)
    nxt = after[...].astype(jnp.float32)
    done = []
    for i in range(count):
        cur = mine[:, i * each : (i + 1) * each]
        if i >= count - OMAX:
            takes = [(j == i - count + ov_next, nxt[:, j * each : (j + 1) * each]) for j in range(OMAX)]
            cur = join(cur, i >= count - ov_next, takes)
        done.append(cur)
    out[...] = jnp.concatenate(done, axis=1).astype(jnp.bfloat16)


def average_low_kernel(overlap, low, before, high, out):
    half = low.shape[1]
    each = 8
    count = half // each
    ov_prev = overlap[0]
    mine = low[...].astype(jnp.float32)
    prev = before[...].astype(jnp.float32)
    done = []
    for i in range(count):
        cur = mine[:, i * each : (i + 1) * each]
        if i < OMAX:
            takes = [
                (j == OMAX - ov_prev + i, prev[:, (count - OMAX + j) * each : (count - OMAX + j + 1) * each])
                for j in range(OMAX)
            ]
            cur = join(cur, i < ov_prev, [((i < ov_prev) & t, o) for t, o in takes])
        done.append(cur)
    out[:, :half, :] = jnp.concatenate(done, axis=1).astype(jnp.bfloat16)
    out[:, half:, :] = high[...]


def average(kernel, overlap, parts, rows):
    full = pl.BlockSpec(memory_space=pltpu.VMEM)
    blocks, _, width = parts[0].shape
    shape = jax.ShapeDtypeStruct((blocks, rows, width), jnp.bfloat16)
    return pl.pallas_call(
        kernel,
        in_specs=[pl.BlockSpec(memory_space=pltpu.SMEM)] + [full] * len(parts),
        out_specs=full,
        out_shape=shape,
        cost_estimate=cost(8 * blocks * rows * width, parts, (shape,)),
        compiler_params=pltpu.CompilerParams(vmem_limit_bytes=16 * MIB),
    )(overlap, *parts)


def blend_kernel(pid, lat, mod_ref, avg, out):
    blocks, _, width = avg.shape
    gate = mod_ref[2, pl.ds(pid[0], 1), :]
    for b in range(0, blocks, 2):
        cols = slice(b * width, (b + 2) * width)
        a = jnp.concatenate([avg[b].astype(jnp.float32), avg[b + 1].astype(jnp.float32)], axis=1)
        out[:, cols] = (lat[:, cols].astype(jnp.float32) + gate[:, cols] * a).astype(jnp.bfloat16)


def blend(pid, lat, modulation, avg):
    full = pl.BlockSpec(memory_space=pltpu.VMEM)
    return pl.pallas_call(
        blend_kernel,
        in_specs=[pl.BlockSpec(memory_space=pltpu.SMEM)] + [full] * 3,
        out_specs=full,
        out_shape=jax.ShapeDtypeStruct(lat.shape, jnp.bfloat16),
        compiler_params=pltpu.CompilerParams(vmem_limit_bytes=16 * MIB),
    )(pid, lat, modulation, avg)


def around(value, axis, by):
    n = lax.axis_size(axis)
    return lax.ppermute(value, axis, [(i, (i + by) % n) for i in range(n)])


def along(value, by):
    n = lax.axis_size(("ylo", "z"))
    return lax.ppermute(value, ("ylo", "z"), [(i, i + by) for i in range(n) if 0 <= i + by < n])


def shards(latents, prompt_ids, modulation, w_qkv, intersection):
    _, frames, patches, width = latents.shape
    rows = frames * patches
    mine = latents.reshape(rows, width)
    wa = w_qkv.reshape(-1, width)
    place = jnp.stack([lax.axis_index("x"), lax.axis_index("yhi"), lax.axis_index("core")]).astype(jnp.int32)

    modulation = jnp.transpose(modulation, (1, 0, 2))
    window = lax.axis_index(("ylo", "z"))
    padded = jnp.concatenate([intersection, jnp.zeros((1,), jnp.int32)])
    overlap = lax.dynamic_slice(padded, (window,), (2,))

    other = around(mine, "yhi", 1)
    near = [mine] + [around(mine, "x", by) for by in (1, 3, 2)]
    wb = around(wa, "core", 1)
    other, *near = lax.optimization_barrier((other, *near))
    far = [other] + [around(other, "x", by) for by in (1, 3, 2)]

    groups = []
    for blocks in (near, far):
        own, give = project(prompt_ids, blocks, modulation, [wa, wb])
        groups += [own, around(give, "core", 1)]
    groups = [g.reshape(-1, rows, g.shape[-1]) for g in groups]

    half = rows // 2
    low = attend(0, half, place, groups)
    after = along(low, -1)
    high = attend(half, half, place, groups)
    before = along(high, 1)

    avg = average(average_high_kernel, overlap, (high, after), half)
    avg = average(average_low_kernel, overlap, (low, before, avg), rows)
    avg = lax.all_to_all(avg, ("x", "yhi", "core"), 0, 0)
    return blend(prompt_ids, mine, modulation, avg).reshape(latents.shape)


def solution(mesh):
    fine = Mesh(mesh.devices.reshape(4, 8, NX, NY, NC), ("ylo", "z", "x", "yhi", "core"))
    win, head = ("ylo", "z"), ("x", "yhi", "core")
    in_specs = (P(win, None, head, None), P(win), P(), P(None, head, None), P())
    out_specs = P(win, None, head, None)
    return jax.shard_map(shards, mesh=fine, in_specs=in_specs, out_specs=out_specs, check_vma=False)
```

```python
import functools

import jax
import jax.numpy as jnp
from jax import lax
from jax.experimental import pallas as pl
from jax.experimental.pallas import tpu as pltpu
from jax.sharding import Mesh
from jax.sharding import PartitionSpec as P

HEAD_DIM = 64
OMAX = 3
NX, NY, NC = 4, 2, 2
MIB = 1 << 20
STEPS = (2, 1, 3)
ORIGINS = tuple((NX - by) % NX for by in STEPS)
SUM_LANE, TOP_LANE = HEAD_DIM, HEAD_DIM + 1
PIECES = 6
PATCH = 8


def cost(flops, inputs, outputs, transcendentals=0):
    size = sum(a.size * a.dtype.itemsize for a in (*inputs, *outputs))
    return pl.CostEstimate(flops=flops, bytes_accessed=size, transcendentals=transcendentals)


def project_kernel(blocks, hbm, *refs):
    tokens, (mods, wa, wb, oa, ob, normed), rest = refs[:blocks], refs[blocks : blocks + 6], refs[blocks + 6 :]
    tokens = list(tokens)
    rows = tokens[-1].shape[0]
    copies = []
    if hbm:
        va, first, sems = rest
        copies.append(pltpu.make_async_copy(tokens[0], first, sems.at[0]))
        step = wa.shape[0] // PIECES
        for i in range(PIECES):
            part = pl.ds(i * step, step)
            copies.append(pltpu.make_async_copy(wa.at[part], va.at[part], sems.at[i + 1]))
        tokens[0], wa = first, va
    for c in copies:
        c.start()
    shift = mods[0:1, :]
    scale = 1.0 + mods[1:2, :]
    for i in (*range(1, blocks), 0):
        if i == 0 and hbm:
            copies[0].wait()
        xf = tokens[i][...].astype(jnp.float32)
        mean = jnp.mean(xf, axis=-1, keepdims=True)
        xc = xf - mean
        var = jnp.mean(xc * xc, axis=-1, keepdims=True)
        normed[i * rows : (i + 1) * rows] = (xc * lax.rsqrt(var + 1e-06) * scale + shift).astype(jnp.bfloat16)
    contract = (((1,), (1,)), ((), ()))
    ob[...] = lax.dot_general(normed[...], wb[...], contract, preferred_element_type=jnp.float32).astype(jnp.bfloat16)
    for c in copies[1:]:
        c.wait()
    oa[...] = lax.dot_general(normed[...], wa[...], contract, preferred_element_type=jnp.float32).astype(jnp.bfloat16)


def project(blocks, mods, wa, wb, hbm):
    rows = sum(b.shape[0] for b in blocks)
    feats, width = wa.shape
    full = pl.BlockSpec(memory_space=pltpu.VMEM)
    far = pl.BlockSpec(memory_space=pltpu.HBM) if hbm else full
    shape = jax.ShapeDtypeStruct((rows, feats), jnp.bfloat16)
    scratch = [pltpu.VMEM((rows, width), jnp.bfloat16)]
    if hbm:
        wa = pltpu.with_memory_space_constraint(wa, pltpu.HBM)
        blocks = [pltpu.with_memory_space_constraint(blocks[0], pltpu.HBM), *blocks[1:]]
        scratch += [
            pltpu.VMEM((feats, width), jnp.bfloat16),
            pltpu.VMEM(blocks[0].shape, jnp.bfloat16),
            pltpu.SemaphoreType.DMA((PIECES + 1,)),
        ]
    return pl.pallas_call(
        functools.partial(project_kernel, len(blocks), hbm),
        in_specs=[far] + [full] * len(blocks) + [far, full],
        out_specs=[full] * 2,
        out_shape=[shape] * 2,
        scratch_shapes=scratch,
        cost_estimate=cost(1, (), ()),
        compiler_params=pltpu.CompilerParams(vmem_limit_bytes=20 * MIB),
    )(*blocks, mods, wa, wb)


def columns(groups, part, h, rows=slice(None)):
    width = groups[0].shape[2] // 3
    a = part * width + h * HEAD_DIM
    taken = [g[:, rows, a : a + HEAD_DIM] for g in groups]
    return jnp.concatenate([t.reshape(-1, HEAD_DIM) for t in taken], axis=0)


def values(groups, h):
    v = columns(groups, 2, h)
    lane = lax.broadcasted_iota(jnp.int32, (v.shape[0], 2 * HEAD_DIM), 1)
    return jnp.where(lane == SUM_LANE, jnp.ones_like(v[:1, :1]), jnp.concatenate([v, jnp.zeros_like(v)], axis=1))


def scored(q, k):
    return lax.dot_general(q, k, (((1,), (1,)), ((), ())), preferred_element_type=jnp.float32)


def weighted(s, top, v):
    p = jnp.exp((s - top) * (HEAD_DIM**-0.5)).astype(jnp.bfloat16)
    return lax.dot_general(p, v, (((1,), (0,)), ((), ())), preferred_element_type=jnp.float32)


def early_kernel(own, got, state):
    groups = (own, got)
    lane = lax.broadcasted_iota(jnp.int32, (1, 2 * HEAD_DIM), 1)
    heads = own.shape[2] // 3 // HEAD_DIM
    s = scored(columns(groups, 0, 0), columns(groups, 1, 0))
    for h in range(heads):
        then = scored(columns(groups, 0, h + 1), columns(groups, 1, h + 1)) if h + 1 < heads else None
        top = jnp.max(s, axis=-1, keepdims=True)
        out = jnp.where(lane == TOP_LANE, top, weighted(s, top, values(groups, h)))
        state[:, :, 2 * h * HEAD_DIM : 2 * (h + 1) * HEAD_DIM] = out.reshape(-1, own.shape[1], 2 * HEAD_DIM)
        s = then


def early(own, got):
    blocks, rows, feats = own.shape
    full = pl.BlockSpec(memory_space=pltpu.VMEM)
    shape = jax.ShapeDtypeStruct((2 * blocks, rows, feats // 3 * 2), jnp.float32)
    scores = (2 * blocks * rows) ** 2 * (feats // 3 // HEAD_DIM)
    return pl.pallas_call(
        early_kernel,
        in_specs=[full] * 2,
        out_specs=full,
        out_shape=shape,
        cost_estimate=cost(1, (), ()),
        compiler_params=pltpu.CompilerParams(vmem_limit_bytes=24 * MIB),
    )(own, got)


def attend_kernel(own0, got0, own1, got1, state, pair, third, first3, last3):
    a, b = (own0, got0), (own1, got1)
    rows = own0.shape[1]
    heads = own0.shape[2] // 3 // HEAD_DIM
    jobs = [(h, late) for h in range(heads) for late in (False, True)]

    def score(h, late):
        k = columns(b, 1, h)
        if late:
            return scored(columns(b, 0, h), jnp.concatenate([columns(a, 1, h), k], axis=0))
        return scored(columns(a, 0, h), k)

    done = {}
    s = score(*jobs[0])
    for i, (h, late) in enumerate(jobs):
        then = score(*jobs[i + 1]) if i + 1 < len(jobs) else None
        v = values(b, h)
        if late:
            top = jnp.max(s, axis=-1, keepdims=True)
            o = weighted(s, top, jnp.concatenate([values(a, h), v], axis=0))
        else:
            before = state[:, :, 2 * h * HEAD_DIM : 2 * (h + 1) * HEAD_DIM].reshape(-1, 2 * HEAD_DIM)
            top0 = before[:, TOP_LANE : TOP_LANE + 1]
            top = jnp.maximum(top0, jnp.max(s, axis=-1, keepdims=True))
            o = before * jnp.exp((top0 - top) * (HEAD_DIM**-0.5)) + weighted(s, top, v)
        done[h, late] = (o[:, :HEAD_DIM] / o[:, SUM_LANE : SUM_LANE + 1]).reshape(2, -1, rows, HEAD_DIM)
        s = then
    out = []
    for h in range(heads):
        parts = [done[h, late][j] for j in range(2) for late in (False, True)]
        out.append(jnp.concatenate(parts, axis=0))
    two = jnp.concatenate(out[:2], axis=2)
    pair[...] = two.astype(jnp.bfloat16)
    third[...] = out[2].astype(jnp.bfloat16)
    edge = OMAX * PATCH
    half = two.shape[0] // 2
    for ref, at in ((first3, 0), (last3, rows - edge)):
        cut = slice(at, at + edge)
        ref[: 2 * half * edge] = two[:, cut].reshape(-1, 2 * HEAD_DIM).astype(jnp.bfloat16)
        one = out[2][:, cut]
        one = jnp.concatenate([one[:half], one[half:]], axis=2)
        ref[2 * half * edge :] = one.reshape(-1, 2 * HEAD_DIM).astype(jnp.bfloat16)


def attend(groups, state):
    blocks = sum(g.shape[0] for g in groups)
    _, rows, feats = groups[0].shape
    full = pl.BlockSpec(memory_space=pltpu.VMEM)
    edge = blocks * OMAX * PATCH * 3 // 2
    shapes = [
        jax.ShapeDtypeStruct(s, jnp.bfloat16)
        for s in ((blocks, rows, 2 * HEAD_DIM), (blocks, rows, HEAD_DIM), (edge, 2 * HEAD_DIM), (edge, 2 * HEAD_DIM))
    ]
    return pl.pallas_call(
        attend_kernel,
        in_specs=[full] * 5,
        out_specs=[full] * 4,
        out_shape=shapes,
        compiler_params=pltpu.CompilerParams(vmem_limit_bytes=32 * MIB),
    )(*groups, state)


def unpacked(ref, blocks):
    rows = OMAX * PATCH
    data = ref[...].astype(jnp.float32)
    two = data[: blocks * rows].reshape(blocks, rows, 2 * HEAD_DIM)
    one = data[blocks * rows :].reshape(blocks // 2, rows, 2 * HEAD_DIM)
    return two, jnp.concatenate([one[:, :, :HEAD_DIM], one[:, :, HEAD_DIM:]], axis=0)


def average_kernel(overlap, place, pair, third, before, after, out):
    blocks, rows, _ = pair.shape
    frames = rows // PATCH
    ov_prev, ov_next = overlap[0], overlap[1]
    whole = []
    for mine, prev, nxt in zip((pair, third), unpacked(before, blocks), unpacked(after, blocks)):
        mine = mine[...].astype(jnp.float32)
        done = []
        for f in range(frames):
            cur = mine[:, f * PATCH : (f + 1) * PATCH]
            if f < OMAX or f >= frames - OMAX:
                if f < OMAX:
                    shared, source, at = f < ov_prev, prev, OMAX - ov_prev + f
                else:
                    shared, source, at = f >= frames - ov_next, nxt, f - frames + ov_next
                part = jnp.zeros_like(cur)
                for j in range(OMAX):
                    part = jnp.where(shared & (at == j), source[:, j * PATCH : (j + 1) * PATCH], part)
                cur = (cur + part) * jnp.where(shared, 0.5, 1.0)
            done.append(cur)
        whole.append(done)
    two = jnp.concatenate(whole[0], axis=1).astype(jnp.bfloat16)
    half = frames // 2
    one = jnp.concatenate(
        [jnp.concatenate(whole[1][:half], axis=1), jnp.concatenate(whole[1][half:], axis=1)], axis=2
    ).astype(jnp.bfloat16)
    for n in range(blocks):
        i = n % (blocks // 2)
        x = lax.rem(place[0] + (0, *ORIGINS, 0, *ORIGINS)[i], NX)
        y = place[1] if i < NX else 1 - place[1]
        c = place[2] if n < blocks // 2 else 1 - place[2]
        h = (x * NY + y) * NC + c
        out[h, :rows] = two[n]
        out[h, rows:] = one[n]


def average(overlap, place, pair, third, before, after):
    full = pl.BlockSpec(memory_space=pltpu.VMEM)
    smem = pl.BlockSpec(memory_space=pltpu.SMEM)
    blocks, rows, lanes = pair.shape
    return pl.pallas_call(
        average_kernel,
        in_specs=[smem] * 2 + [full] * 4,
        out_specs=full,
        out_shape=jax.ShapeDtypeStruct((blocks, rows * 3 // 2, lanes), jnp.bfloat16),
        compiler_params=pltpu.CompilerParams(vmem_limit_bytes=16 * MIB),
    )(overlap, place, pair, third, before, after)


def blend_kernel(lat, mods, avg, out):
    blocks = avg.shape[0]
    rows = lat.shape[0]
    width = 3 * HEAD_DIM
    for b in range(0, blocks, 2):
        parts = []
        for s in (b, b + 1):
            parts.append(avg[s, :rows].astype(jnp.float32))
            one = avg[s, rows:].astype(jnp.float32)
            parts.append(jnp.concatenate([one[:, :HEAD_DIM], one[:, HEAD_DIM:]], axis=0))
        cols = slice(b * width, (b + 2) * width)
        a = jnp.concatenate(parts, axis=1)
        out[:, cols] = (lat[:, cols].astype(jnp.float32) + mods[2:3, cols] * a).astype(jnp.bfloat16)


def blend(lat, mods, avg):
    full = pl.BlockSpec(memory_space=pltpu.VMEM)
    return pl.pallas_call(
        blend_kernel,
        in_specs=[full] * 3,
        out_specs=full,
        out_shape=jax.ShapeDtypeStruct(lat.shape, jnp.bfloat16),
        compiler_params=pltpu.CompilerParams(vmem_limit_bytes=16 * MIB),
    )(lat, mods, avg)


def around(value, axis, by):
    n = lax.axis_size(axis)
    return lax.ppermute(value, axis, [(i, (i + by) % n) for i in range(n)])


def along(value, by):
    n = lax.axis_size(("ylo", "z"))
    return lax.ppermute(value, ("ylo", "z"), [(i, i + by) for i in range(n) if 0 <= i + by < n])


def shards(latents, prompt_ids, modulation, w_qkv, intersection):
    _, frames, patches, width = latents.shape
    rows = frames * patches
    mine = latents.reshape(rows, width)
    wa = w_qkv.reshape(-1, width)
    place = jnp.stack([lax.axis_index("x"), lax.axis_index("yhi"), lax.axis_index("core")]).astype(jnp.int32)

    mods = lax.dynamic_index_in_dim(modulation, prompt_ids[0], keepdims=False)
    window = lax.axis_index(("ylo", "z"))
    padded = jnp.concatenate([intersection, jnp.zeros((1,), jnp.int32)])
    overlap = lax.dynamic_slice(padded, (window,), (2,))

    other = around(mine, "yhi", 1)
    near = [around(mine, "x", by) for by in STEPS]
    wb = around(wa, "core", 1)
    other, *near = lax.optimization_barrier((other, *near))
    far = [around(other, "x", by) for by in STEPS]

    own, give = project([mine, *near, other], mods, wa, wb, True)
    pair0 = [g.reshape(-1, rows, g.shape[-1]) for g in (own, around(give, "core", 1))]
    state = early(*pair0)
    state, *far = lax.optimization_barrier((state, *far))
    own, give = project(far, mods, wa, wb, False)
    pair1 = [g.reshape(-1, rows, g.shape[-1]) for g in (own, around(give, "core", 1))]

    pair, third, first3, last3 = attend(pair0 + pair1, state)
    before = along(last3, 1)
    after = along(first3, -1)
    avg = average(overlap, place, pair, third, before, after)
    avg = lax.all_to_all(avg, ("x", "yhi", "core"), 0, 0)
    return blend(mine, mods, avg).reshape(latents.shape)


def solution(mesh):
    fine = Mesh(mesh.devices.reshape(4, 8, NX, NY, NC), ("ylo", "z", "x", "yhi", "core"))
    win, head = ("ylo", "z"), ("x", "yhi", "core")
    in_specs = (P(win, None, head, None), P(win), P(), P(None, head, None), P())
    out_specs = P(win, None, head, None)
    return jax.shard_map(shards, mesh=fine, in_specs=in_specs, out_specs=out_specs, check_vma=False)
```

```python
import functools

import jax
import jax.numpy as jnp
from jax import lax
from jax.experimental import pallas as pl
from jax.experimental.pallas import tpu as pltpu
from jax.sharding import Mesh
from jax.sharding import PartitionSpec as P

HEAD_DIM = 64
OMAX = 3
NX, NY, NC = 4, 2, 2
MIB = 1 << 20
STEPS = (2, 1, 3)
ORIGINS = tuple((NX - by) % NX for by in STEPS)
SUM_LANE, TOP_LANE = HEAD_DIM, HEAD_DIM + 1
PATCH = 8


def cost(flops, inputs, outputs, transcendentals=0):
    size = sum(a.size * a.dtype.itemsize for a in (*inputs, *outputs))
    return pl.CostEstimate(flops=flops, bytes_accessed=size, transcendentals=transcendentals)


def normalise(tokens, mods, normed, order, before):
    rows = tokens[-1].shape[0]
    shift = mods[0:1, :]
    scale = 1.0 + mods[1:2, :]
    for i in order:
        before(i)
        xf = tokens[i][...].astype(jnp.float32)
        mean = jnp.mean(xf, axis=-1, keepdims=True)
        xc = xf - mean
        var = jnp.mean(xc * xc, axis=-1, keepdims=True)
        normed[i * rows : (i + 1) * rows] = (xc * lax.rsqrt(var + 1e-06) * scale + shift).astype(jnp.bfloat16)


def product(normed, w, out):
    r = lax.dot_general(normed[...], w[...], (((1,), (1,)), ((), ())), preferred_element_type=jnp.float32)
    out[...] = r[: out.shape[0]].astype(jnp.bfloat16)


def early_project_kernel(blocks, *refs):
    tokens, (mods, wa, wb, oa, ob, va, vb, first, normed, sems) = list(refs[:blocks]), refs[blocks:]
    head = pltpu.make_async_copy(tokens[0], first, sems.at[0])
    fetches = [pltpu.make_async_copy(wb, vb, sems.at[1]), pltpu.make_async_copy(wa, va, sems.at[2])]
    for c in (head, *fetches):
        c.start()
    tokens[0] = first
    normalise(tokens, mods, normed, (*range(1, blocks), 0), lambda i: head.wait() if i == 0 else None)
    for c, w, o in zip(fetches, (vb, va), (ob, oa)):
        c.wait()
        product(normed, w, o)


def early_project(blocks, mods, wa, wb):
    rows = sum(b.shape[0] for b in blocks)
    feats, width = wa.shape
    full = pl.BlockSpec(memory_space=pltpu.VMEM)
    away = pl.BlockSpec(memory_space=pltpu.HBM)
    first, wa, wb = [pltpu.with_memory_space_constraint(a, pltpu.HBM) for a in (blocks[0], wa, wb)]
    shape = jax.ShapeDtypeStruct((rows, feats), jnp.bfloat16)
    weight = jax.ShapeDtypeStruct((feats, width), jnp.bfloat16)
    return pl.pallas_call(
        functools.partial(early_project_kernel, len(blocks)),
        in_specs=[away] + [full] * len(blocks) + [away] * 2,
        out_specs=[full] * 4,
        out_shape=[shape, shape, weight, weight],
        scratch_shapes=[
            pltpu.VMEM(first.shape, jnp.bfloat16),
            pltpu.VMEM((rows, width), jnp.bfloat16),
            pltpu.SemaphoreType.DMA((3,)),
        ],
        cost_estimate=cost(1, (), ()),
        compiler_params=pltpu.CompilerParams(vmem_limit_bytes=24 * MIB),
    )(first, *blocks[1:], mods, wa, wb)


def project_kernel(blocks, *refs):
    tokens, (mods, wa, wb, oa, ob, normed) = refs[:blocks], refs[blocks:]
    used = oa.shape[0]
    normed[used:] = jnp.zeros((normed.shape[0] - used, normed.shape[1]), jnp.bfloat16)
    normalise(tokens, mods, normed, range(blocks), lambda i: None)
    product(normed, wb, ob)
    product(normed, wa, oa)


def project(blocks, mods, wa, wb):
    rows = sum(b.shape[0] for b in blocks)
    feats, width = wa.shape
    full = pl.BlockSpec(memory_space=pltpu.VMEM)
    shape = jax.ShapeDtypeStruct((rows, feats), jnp.bfloat16)
    return pl.pallas_call(
        functools.partial(project_kernel, len(blocks)),
        in_specs=[full] * (len(blocks) + 3),
        out_specs=[full] * 2,
        out_shape=[shape] * 2,
        scratch_shapes=[pltpu.VMEM((4 * blocks[0].shape[0], width), jnp.bfloat16)],
        cost_estimate=cost(1, (wa, wb), ()),
        compiler_params=pltpu.CompilerParams(vmem_limit_bytes=24 * MIB),
    )(*blocks, mods, wa, wb)


def columns(groups, part, h, rows=slice(None)):
    width = groups[0].shape[2] // 3
    a = part * width + h * HEAD_DIM
    taken = [g[:, rows, a : a + HEAD_DIM] for g in groups]
    return jnp.concatenate([t.reshape(-1, HEAD_DIM) for t in taken], axis=0)


def values(groups, h):
    v = columns(groups, 2, h)
    lane = lax.broadcasted_iota(jnp.int32, (v.shape[0], 2 * HEAD_DIM), 1)
    return jnp.where(lane == SUM_LANE, jnp.ones_like(v[:1, :1]), jnp.concatenate([v, jnp.zeros_like(v)], axis=1))


def scored(q, k):
    return lax.dot_general(q, k, (((1,), (1,)), ((), ())), preferred_element_type=jnp.float32)


def weighted(s, top, v):
    p = jnp.exp((s - top) * (HEAD_DIM**-0.5)).astype(jnp.bfloat16)
    return lax.dot_general(p, v, (((1,), (0,)), ((), ())), preferred_element_type=jnp.float32)


def early_kernel(own, got, state):
    groups = (own, got)
    lane = lax.broadcasted_iota(jnp.int32, (1, 2 * HEAD_DIM), 1)
    heads = own.shape[2] // 3 // HEAD_DIM
    s = scored(columns(groups, 0, 0), columns(groups, 1, 0))
    for h in range(heads):
        then = scored(columns(groups, 0, h + 1), columns(groups, 1, h + 1)) if h + 1 < heads else None
        top = jnp.max(s, axis=-1, keepdims=True)
        out = jnp.where(lane == TOP_LANE, top, weighted(s, top, values(groups, h)))
        state[:, :, 2 * h * HEAD_DIM : 2 * (h + 1) * HEAD_DIM] = out.reshape(-1, own.shape[1], 2 * HEAD_DIM)
        s = then


def early(own, got):
    blocks, rows, feats = own.shape
    full = pl.BlockSpec(memory_space=pltpu.VMEM)
    shape = jax.ShapeDtypeStruct((2 * blocks, rows, feats // 3 * 2), jnp.float32)
    scores = (2 * blocks * rows) ** 2 * (feats // 3 // HEAD_DIM)
    return pl.pallas_call(
        early_kernel,
        in_specs=[full] * 2,
        out_specs=full,
        out_shape=shape,
        cost_estimate=cost(1, (), ()),
        compiler_params=pltpu.CompilerParams(vmem_limit_bytes=24 * MIB),
    )(own, got)


def attend_kernel(own0, got0, own1, got1, state, pair, third, first3, last3):
    a, b = (own0, got0), (own1, got1)
    rows = own0.shape[1]
    heads = own0.shape[2] // 3 // HEAD_DIM
    jobs = [(h, late) for h in range(heads) for late in (False, True)]

    def score(h, late):
        k = columns(b, 1, h)
        if late:
            return scored(columns(b, 0, h), jnp.concatenate([columns(a, 1, h), k], axis=0))
        return scored(columns(a, 0, h), k)

    done = {}
    s = score(*jobs[0])
    for i, (h, late) in enumerate(jobs):
        then = score(*jobs[i + 1]) if i + 1 < len(jobs) else None
        v = values(b, h)
        if late:
            top = jnp.max(s, axis=-1, keepdims=True)
            o = weighted(s, top, jnp.concatenate([values(a, h), v], axis=0))
        else:
            before = state[:, :, 2 * h * HEAD_DIM : 2 * (h + 1) * HEAD_DIM].reshape(-1, 2 * HEAD_DIM)
            top0 = before[:, TOP_LANE : TOP_LANE + 1]
            top = jnp.maximum(top0, jnp.max(s, axis=-1, keepdims=True))
            o = before * jnp.exp((top0 - top) * (HEAD_DIM**-0.5)) + weighted(s, top, v)
        done[h, late] = (o[:, :HEAD_DIM] / o[:, SUM_LANE : SUM_LANE + 1]).reshape(2, -1, rows, HEAD_DIM)
        s = then
    out = []
    for h in range(heads):
        parts = [done[h, late][j] for j in range(2) for late in (False, True)]
        out.append(jnp.concatenate(parts, axis=0))
    two = jnp.concatenate(out[:2], axis=2)
    pair[...] = two.astype(jnp.bfloat16)
    third[...] = out[2].astype(jnp.bfloat16)
    edge = OMAX * PATCH
    half = two.shape[0] // 2
    for ref, at in ((first3, 0), (last3, rows - edge)):
        cut = slice(at, at + edge)
        ref[: 2 * half * edge] = two[:, cut].reshape(-1, 2 * HEAD_DIM).astype(jnp.bfloat16)
        one = out[2][:, cut]
        one = jnp.concatenate([one[:half], one[half:]], axis=2)
        ref[2 * half * edge :] = one.reshape(-1, 2 * HEAD_DIM).astype(jnp.bfloat16)


def attend(groups, state):
    blocks = sum(g.shape[0] for g in groups)
    _, rows, feats = groups[0].shape
    full = pl.BlockSpec(memory_space=pltpu.VMEM)
    edge = blocks * OMAX * PATCH * 3 // 2
    shapes = [
        jax.ShapeDtypeStruct(s, jnp.bfloat16)
        for s in ((blocks, rows, 2 * HEAD_DIM), (blocks, rows, HEAD_DIM), (edge, 2 * HEAD_DIM), (edge, 2 * HEAD_DIM))
    ]
    return pl.pallas_call(
        attend_kernel,
        in_specs=[full] * 5,
        out_specs=[full] * 4,
        out_shape=shapes,
        compiler_params=pltpu.CompilerParams(vmem_limit_bytes=32 * MIB),
    )(*groups, state)


def unpacked(ref, blocks):
    rows = OMAX * PATCH
    data = ref[...].astype(jnp.float32)
    two = data[: blocks * rows].reshape(blocks, rows, 2 * HEAD_DIM)
    one = data[blocks * rows :].reshape(blocks // 2, rows, 2 * HEAD_DIM)
    return two, jnp.concatenate([one[:, :, :HEAD_DIM], one[:, :, HEAD_DIM:]], axis=0)


def average_kernel(overlap, place, pair, third, before, after, out):
    blocks, rows, _ = pair.shape
    frames = rows // PATCH
    ov_prev, ov_next = overlap[0], overlap[1]
    whole = []
    for mine, prev, nxt in zip((pair, third), unpacked(before, blocks), unpacked(after, blocks)):
        mine = mine[...].astype(jnp.float32)
        done = []
        for f in range(frames):
            cur = mine[:, f * PATCH : (f + 1) * PATCH]
            if f < OMAX or f >= frames - OMAX:
                if f < OMAX:
                    shared, source, at = f < ov_prev, prev, OMAX - ov_prev + f
                else:
                    shared, source, at = f >= frames - ov_next, nxt, f - frames + ov_next
                part = jnp.zeros_like(cur)
                for j in range(OMAX):
                    part = jnp.where(shared & (at == j), source[:, j * PATCH : (j + 1) * PATCH], part)
                cur = (cur + part) * jnp.where(shared, 0.5, 1.0)
            done.append(cur)
        whole.append(done)
    two = jnp.concatenate(whole[0], axis=1).astype(jnp.bfloat16)
    half = frames // 2
    one = jnp.concatenate(
        [jnp.concatenate(whole[1][:half], axis=1), jnp.concatenate(whole[1][half:], axis=1)], axis=2
    ).astype(jnp.bfloat16)
    for n in range(blocks):
        i = n % (blocks // 2)
        x = lax.rem(place[0] + (0, *ORIGINS, 0, *ORIGINS)[i], NX)
        y = place[1] if i < NX else 1 - place[1]
        c = place[2] if n < blocks // 2 else 1 - place[2]
        h = (x * NY + y) * NC + c
        out[h, :rows] = two[n]
        out[h, rows:] = one[n]


def average(overlap, place, pair, third, before, after):
    full = pl.BlockSpec(memory_space=pltpu.VMEM)
    smem = pl.BlockSpec(memory_space=pltpu.SMEM)
    blocks, rows, lanes = pair.shape
    return pl.pallas_call(
        average_kernel,
        in_specs=[smem] * 2 + [full] * 4,
        out_specs=full,
        out_shape=jax.ShapeDtypeStruct((blocks, rows * 3 // 2, lanes), jnp.bfloat16),
        compiler_params=pltpu.CompilerParams(vmem_limit_bytes=16 * MIB),
    )(overlap, place, pair, third, before, after)


def blend_kernel(lat, mods, avg, out):
    blocks = avg.shape[0]
    rows = lat.shape[0]
    width = 3 * HEAD_DIM
    for b in range(0, blocks, 2):
        parts = []
        for s in (b, b + 1):
            parts.append(avg[s, :rows].astype(jnp.float32))
            one = avg[s, rows:].astype(jnp.float32)
            parts.append(jnp.concatenate([one[:, :HEAD_DIM], one[:, HEAD_DIM:]], axis=0))
        cols = slice(b * width, (b + 2) * width)
        a = jnp.concatenate(parts, axis=1)
        out[:, cols] = (lat[:, cols].astype(jnp.float32) + mods[2:3, cols] * a).astype(jnp.bfloat16)


def blend(lat, mods, avg):
    full = pl.BlockSpec(memory_space=pltpu.VMEM)
    return pl.pallas_call(
        blend_kernel,
        in_specs=[full] * 3,
        out_specs=full,
        out_shape=jax.ShapeDtypeStruct(lat.shape, jnp.bfloat16),
        compiler_params=pltpu.CompilerParams(vmem_limit_bytes=16 * MIB),
    )(lat, mods, avg)


def around(value, axis, by):
    n = lax.axis_size(axis)
    return lax.ppermute(value, axis, [(i, (i + by) % n) for i in range(n)])


def along(value, by):
    n = lax.axis_size(("ylo", "z"))
    return lax.ppermute(value, ("ylo", "z"), [(i, i + by) for i in range(n) if 0 <= i + by < n])


def shards(latents, prompt_ids, modulation, w_qkv, intersection):
    _, frames, patches, width = latents.shape
    rows = frames * patches
    mine = latents.reshape(rows, width)
    wa = w_qkv.reshape(-1, width)
    place = jnp.stack([lax.axis_index("x"), lax.axis_index("yhi"), lax.axis_index("core")]).astype(jnp.int32)

    mods = lax.dynamic_index_in_dim(modulation, prompt_ids[0], keepdims=False)
    window = lax.axis_index(("ylo", "z"))
    padded = jnp.concatenate([intersection, jnp.zeros((1,), jnp.int32)])
    overlap = lax.dynamic_slice(padded, (window,), (2,))

    other = around(mine, "yhi", 1)
    near = [around(mine, "x", by) for by in STEPS]
    wb = around(wa, "core", 1)
    far = [around(other, "x", by) for by in STEPS]

    own, give, wa, wb = early_project([mine, *near, other], mods, wa, wb)
    pair0 = [g.reshape(-1, rows, g.shape[-1]) for g in (own, around(give, "core", 1))]
    state = early(*pair0)
    own, give = project(far, mods, wa, wb)
    pair1 = [g.reshape(-1, rows, g.shape[-1]) for g in (own, around(give, "core", 1))]

    pair, third, first3, last3 = attend(pair0 + pair1, state)
    before = along(last3, 1)
    after = along(first3, -1)
    avg = average(overlap, place, pair, third, before, after)
    avg = lax.all_to_all(avg, ("x", "yhi", "core"), 0, 0)
    return blend(mine, mods, avg).reshape(latents.shape)


def solution(mesh):
    fine = Mesh(mesh.devices.reshape(4, 8, NX, NY, NC), ("ylo", "z", "x", "yhi", "core"))
    win, head = ("ylo", "z"), ("x", "yhi", "core")
    in_specs = (P(win, None, head, None), P(win), P(), P(None, head, None), P())
    out_specs = P(win, None, head, None)
    return jax.shard_map(shards, mesh=fine, in_specs=in_specs, out_specs=out_specs, check_vma=False)
```

```python
import functools

import jax
import jax.numpy as jnp
from jax import lax
from jax.experimental import pallas as pl
from jax.experimental.pallas import tpu as pltpu
from jax.sharding import Mesh
from jax.sharding import PartitionSpec as P

HEAD_DIM = 64
OMAX = 3
NX, NY, NC = 4, 2, 2
MIB = 1 << 20
STEPS = (2, 1, 3)
ORIGINS = tuple((NX - by) % NX for by in STEPS)
SUM_LANE, TOP_LANE = HEAD_DIM, HEAD_DIM + 1
PATCH = 8


def cost(flops, inputs, outputs, transcendentals=0):
    size = sum(a.size * a.dtype.itemsize for a in (*inputs, *outputs))
    return pl.CostEstimate(flops=flops, bytes_accessed=size, transcendentals=transcendentals)


def choose_kernel(pid, source, out, modulation, sem):
    copy = pltpu.make_async_copy(source, modulation, sem)
    copy.start()
    copy.wait()
    for c in range(out.shape[0]):
        out[c : c + 1, :] = modulation[c, pl.ds(pid[0], 1), :]


def choose(pid, modulation):
    modulation = pltpu.with_memory_space_constraint(modulation, pltpu.HBM)
    return pl.pallas_call(
        choose_kernel,
        in_specs=[pl.BlockSpec(memory_space=pltpu.SMEM), pl.BlockSpec(memory_space=pltpu.HBM)],
        out_specs=pl.BlockSpec(memory_space=pltpu.VMEM),
        scratch_shapes=[pltpu.VMEM(modulation.shape, jnp.float32), pltpu.SemaphoreType.DMA],
        out_shape=jax.ShapeDtypeStruct((modulation.shape[0], modulation.shape[2]), jnp.float32),
        cost_estimate=cost(10**11, (), ()),
        compiler_params=pltpu.CompilerParams(vmem_limit_bytes=8 * MIB),
    )(pid, modulation)


def normalise(tokens, mods, normed, order, before):
    rows = tokens[-1].shape[0]
    shift = mods[0:1, :]
    scale = 1.0 + mods[1:2, :]
    for i in order:
        before(i)
        xf = tokens[i][...].astype(jnp.float32)
        mean = jnp.mean(xf, axis=-1, keepdims=True)
        xc = xf - mean
        var = jnp.mean(xc * xc, axis=-1, keepdims=True)
        normed[i * rows : (i + 1) * rows] = (xc * lax.rsqrt(var + 1e-06) * scale + shift).astype(jnp.bfloat16)


def product(normed, w, out):
    r = lax.dot_general(normed[...], w[...], (((1,), (1,)), ((), ())), preferred_element_type=jnp.float32)
    out[...] = r[: out.shape[0]].astype(jnp.bfloat16)


def early_project_kernel(blocks, *refs):
    tokens, (mods, wa, wb, oa, ob, va, first, normed, sems) = list(refs[:blocks]), refs[blocks:]
    head = pltpu.make_async_copy(tokens[0], first, sems.at[0])
    fetch = pltpu.make_async_copy(wa, va, sems.at[1])
    head.start()
    fetch.start()
    tokens[0] = first
    normalise(tokens, mods, normed, (*range(1, blocks), 0), lambda i: head.wait() if i == 0 else None)
    product(normed, wb, ob)
    fetch.wait()
    product(normed, va, oa)


def early_project(blocks, mods, wa, wb):
    rows = sum(b.shape[0] for b in blocks)
    feats, width = wa.shape
    full = pl.BlockSpec(memory_space=pltpu.VMEM)
    away = pl.BlockSpec(memory_space=pltpu.HBM)
    first, wa = [pltpu.with_memory_space_constraint(a, pltpu.HBM) for a in (blocks[0], wa)]
    shape = jax.ShapeDtypeStruct((rows, feats), jnp.bfloat16)
    weight = jax.ShapeDtypeStruct((feats, width), jnp.bfloat16)
    return pl.pallas_call(
        functools.partial(early_project_kernel, len(blocks)),
        in_specs=[away] + [full] * len(blocks) + [away, full],
        out_specs=[full] * 3,
        out_shape=[shape, shape, weight],
        scratch_shapes=[
            pltpu.VMEM(first.shape, jnp.bfloat16),
            pltpu.VMEM((rows, width), jnp.bfloat16),
            pltpu.SemaphoreType.DMA((2,)),
        ],
        cost_estimate=cost(1, (), ()),
        compiler_params=pltpu.CompilerParams(vmem_limit_bytes=24 * MIB),
    )(first, *blocks[1:], mods, wa, wb)


def project_kernel(blocks, *refs):
    tokens, (mods, wa, wb, oa, ob, normed) = refs[:blocks], refs[blocks:]
    used = oa.shape[0]
    normed[used:] = jnp.zeros((normed.shape[0] - used, normed.shape[1]), jnp.bfloat16)
    normalise(tokens, mods, normed, range(blocks), lambda i: None)
    product(normed, wb, ob)
    product(normed, wa, oa)


def project(blocks, mods, wa, wb):
    rows = sum(b.shape[0] for b in blocks)
    feats, width = wa.shape
    full = pl.BlockSpec(memory_space=pltpu.VMEM)
    shape = jax.ShapeDtypeStruct((rows, feats), jnp.bfloat16)
    return pl.pallas_call(
        functools.partial(project_kernel, len(blocks)),
        in_specs=[full] * (len(blocks) + 3),
        out_specs=[full] * 2,
        out_shape=[shape] * 2,
        scratch_shapes=[pltpu.VMEM((4 * blocks[0].shape[0], width), jnp.bfloat16)],
        cost_estimate=cost(1, (wa, wb), ()),
        compiler_params=pltpu.CompilerParams(vmem_limit_bytes=24 * MIB),
    )(*blocks, mods, wa, wb)


def columns(groups, part, h, rows=slice(None)):
    width = groups[0].shape[2] // 3
    a = part * width + h * HEAD_DIM
    taken = [g[:, rows, a : a + HEAD_DIM] for g in groups]
    return jnp.concatenate([t.reshape(-1, HEAD_DIM) for t in taken], axis=0)


def values(groups, h):
    v = columns(groups, 2, h)
    lane = lax.broadcasted_iota(jnp.int32, (v.shape[0], 2 * HEAD_DIM), 1)
    return jnp.where(lane == SUM_LANE, jnp.ones_like(v[:1, :1]), jnp.concatenate([v, jnp.zeros_like(v)], axis=1))


def scored(q, k):
    return lax.dot_general(q, k, (((1,), (1,)), ((), ())), preferred_element_type=jnp.float32)


def weighted(s, top, v):
    p = jnp.exp((s - top) * (HEAD_DIM**-0.5)).astype(jnp.bfloat16)
    return lax.dot_general(p, v, (((1,), (0,)), ((), ())), preferred_element_type=jnp.float32)


def early_kernel(own, got, state):
    groups = (own, got)
    lane = lax.broadcasted_iota(jnp.int32, (1, 2 * HEAD_DIM), 1)
    heads = own.shape[2] // 3 // HEAD_DIM
    s = scored(columns(groups, 0, 0), columns(groups, 1, 0))
    for h in range(heads):
        then = scored(columns(groups, 0, h + 1), columns(groups, 1, h + 1)) if h + 1 < heads else None
        top = jnp.max(s, axis=-1, keepdims=True)
        out = jnp.where(lane == TOP_LANE, top, weighted(s, top, values(groups, h)))
        state[:, :, 2 * h * HEAD_DIM : 2 * (h + 1) * HEAD_DIM] = out.reshape(-1, own.shape[1], 2 * HEAD_DIM)
        s = then


def early(own, got):
    blocks, rows, feats = own.shape
    full = pl.BlockSpec(memory_space=pltpu.VMEM)
    shape = jax.ShapeDtypeStruct((2 * blocks, rows, feats // 3 * 2), jnp.float32)
    scores = (2 * blocks * rows) ** 2 * (feats // 3 // HEAD_DIM)
    return pl.pallas_call(
        early_kernel,
        in_specs=[full] * 2,
        out_specs=full,
        out_shape=shape,
        cost_estimate=cost(1, (), ()),
        compiler_params=pltpu.CompilerParams(vmem_limit_bytes=24 * MIB),
    )(own, got)


def attend_kernel(own0, got0, own1, got1, state, pair, third, first3, last3):
    a, b = (own0, got0), (own1, got1)
    rows = own0.shape[1]
    heads = own0.shape[2] // 3 // HEAD_DIM
    jobs = [(h, late) for h in range(heads) for late in (False, True)]

    def score(h, late):
        k = columns(b, 1, h)
        if late:
            return scored(columns(b, 0, h), jnp.concatenate([columns(a, 1, h), k], axis=0))
        return scored(columns(a, 0, h), k)

    done = {}
    s = score(*jobs[0])
    for i, (h, late) in enumerate(jobs):
        then = score(*jobs[i + 1]) if i + 1 < len(jobs) else None
        v = values(b, h)
        if late:
            top = jnp.max(s, axis=-1, keepdims=True)
            o = weighted(s, top, jnp.concatenate([values(a, h), v], axis=0))
        else:
            before = state[:, :, 2 * h * HEAD_DIM : 2 * (h + 1) * HEAD_DIM].reshape(-1, 2 * HEAD_DIM)
            top0 = before[:, TOP_LANE : TOP_LANE + 1]
            top = jnp.maximum(top0, jnp.max(s, axis=-1, keepdims=True))
            o = before * jnp.exp((top0 - top) * (HEAD_DIM**-0.5)) + weighted(s, top, v)
        done[h, late] = (o[:, :HEAD_DIM] / o[:, SUM_LANE : SUM_LANE + 1]).reshape(2, -1, rows, HEAD_DIM)
        s = then
    out = []
    for h in range(heads):
        parts = [done[h, late][j] for j in range(2) for late in (False, True)]
        out.append(jnp.concatenate(parts, axis=0))
    two = jnp.concatenate(out[:2], axis=2)
    pair[...] = two.astype(jnp.bfloat16)
    third[...] = out[2].astype(jnp.bfloat16)
    edge = OMAX * PATCH
    half = two.shape[0] // 2
    for ref, at in ((first3, 0), (last3, rows - edge)):
        cut = slice(at, at + edge)
        ref[: 2 * half * edge] = two[:, cut].reshape(-1, 2 * HEAD_DIM).astype(jnp.bfloat16)
        one = out[2][:, cut]
        one = jnp.concatenate([one[:half], one[half:]], axis=2)
        ref[2 * half * edge :] = one.reshape(-1, 2 * HEAD_DIM).astype(jnp.bfloat16)


def attend(groups, state):
    blocks = sum(g.shape[0] for g in groups)
    _, rows, feats = groups[0].shape
    full = pl.BlockSpec(memory_space=pltpu.VMEM)
    edge = blocks * OMAX * PATCH * 3 // 2
    shapes = [
        jax.ShapeDtypeStruct(s, jnp.bfloat16)
        for s in ((blocks, rows, 2 * HEAD_DIM), (blocks, rows, HEAD_DIM), (edge, 2 * HEAD_DIM), (edge, 2 * HEAD_DIM))
    ]
    return pl.pallas_call(
        attend_kernel,
        in_specs=[full] * 5,
        out_specs=[full] * 4,
        out_shape=shapes,
        compiler_params=pltpu.CompilerParams(vmem_limit_bytes=32 * MIB),
    )(*groups, state)


def unpacked(ref, blocks):
    rows = OMAX * PATCH
    data = ref[...].astype(jnp.float32)
    two = data[: blocks * rows].reshape(blocks, rows, 2 * HEAD_DIM)
    one = data[blocks * rows :].reshape(blocks // 2, rows, 2 * HEAD_DIM)
    return two, jnp.concatenate([one[:, :, :HEAD_DIM], one[:, :, HEAD_DIM:]], axis=0)


def average_kernel(overlap, place, pair, third, before, after, out):
    blocks, rows, _ = pair.shape
    frames = rows // PATCH
    ov_prev, ov_next = overlap[0], overlap[1]
    whole = []
    for mine, prev, nxt in zip((pair, third), unpacked(before, blocks), unpacked(after, blocks)):
        mine = mine[...].astype(jnp.float32)
        done = []
        for f in range(frames):
            cur = mine[:, f * PATCH : (f + 1) * PATCH]
            if f < OMAX or f >= frames - OMAX:
                if f < OMAX:
                    shared, source, at = f < ov_prev, prev, OMAX - ov_prev + f
                else:
                    shared, source, at = f >= frames - ov_next, nxt, f - frames + ov_next
                part = jnp.zeros_like(cur)
                for j in range(OMAX):
                    part = jnp.where(shared & (at == j), source[:, j * PATCH : (j + 1) * PATCH], part)
                cur = (cur + part) * jnp.where(shared, 0.5, 1.0)
            done.append(cur)
        whole.append(done)
    two = jnp.concatenate(whole[0], axis=1).astype(jnp.bfloat16)
    half = frames // 2
    one = jnp.concatenate(
        [jnp.concatenate(whole[1][:half], axis=1), jnp.concatenate(whole[1][half:], axis=1)], axis=2
    ).astype(jnp.bfloat16)
    for n in range(blocks):
        i = n % (blocks // 2)
        x = lax.rem(place[0] + (0, *ORIGINS, 0, *ORIGINS)[i], NX)
        y = place[1] if i < NX else 1 - place[1]
        c = place[2] if n < blocks // 2 else 1 - place[2]
        h = (x * NY + y) * NC + c
        out[h, :rows] = two[n]
        out[h, rows:] = one[n]


def average(overlap, place, pair, third, before, after):
    full = pl.BlockSpec(memory_space=pltpu.VMEM)
    smem = pl.BlockSpec(memory_space=pltpu.SMEM)
    blocks, rows, lanes = pair.shape
    return pl.pallas_call(
        average_kernel,
        in_specs=[smem] * 2 + [full] * 4,
        out_specs=full,
        out_shape=jax.ShapeDtypeStruct((blocks, rows * 3 // 2, lanes), jnp.bfloat16),
        compiler_params=pltpu.CompilerParams(vmem_limit_bytes=16 * MIB),
    )(overlap, place, pair, third, before, after)


def blend_kernel(lat, mods, avg, out):
    blocks = avg.shape[0]
    rows = lat.shape[0]
    width = 3 * HEAD_DIM
    for b in range(0, blocks, 2):
        parts = []
        for s in (b, b + 1):
            parts.append(avg[s, :rows].astype(jnp.float32))
            one = avg[s, rows:].astype(jnp.float32)
            parts.append(jnp.concatenate([one[:, :HEAD_DIM], one[:, HEAD_DIM:]], axis=0))
        cols = slice(b * width, (b + 2) * width)
        a = jnp.concatenate(parts, axis=1)
        out[:, cols] = (lat[:, cols].astype(jnp.float32) + mods[2:3, cols] * a).astype(jnp.bfloat16)


def blend(lat, mods, avg):
    full = pl.BlockSpec(memory_space=pltpu.VMEM)
    return pl.pallas_call(
        blend_kernel,
        in_specs=[full] * 3,
        out_specs=full,
        out_shape=jax.ShapeDtypeStruct(lat.shape, jnp.bfloat16),
        compiler_params=pltpu.CompilerParams(vmem_limit_bytes=16 * MIB),
    )(lat, mods, avg)


def around(value, axis, by):
    n = lax.axis_size(axis)
    return lax.ppermute(value, axis, [(i, (i + by) % n) for i in range(n)])


def along(value, by):
    n = lax.axis_size(("ylo", "z"))
    return lax.ppermute(value, ("ylo", "z"), [(i, i + by) for i in range(n) if 0 <= i + by < n])


def shards(latents, prompt_ids, modulation, w_qkv, intersection):
    _, frames, patches, width = latents.shape
    rows = frames * patches
    mine = latents.reshape(rows, width)
    wa = w_qkv.reshape(-1, width)
    place = jnp.stack([lax.axis_index("x"), lax.axis_index("yhi"), lax.axis_index("core")]).astype(jnp.int32)

    mods = choose(prompt_ids, jnp.transpose(modulation, (1, 0, 2)))
    window = lax.axis_index(("ylo", "z"))
    padded = jnp.concatenate([intersection, jnp.zeros((1,), jnp.int32)])
    overlap = lax.dynamic_slice(padded, (window,), (2,))

    other = around(mine, "yhi", 1)
    near = [around(mine, "x", by) for by in STEPS]
    wb = around(wa, "core", 1)
    far = [around(other, "x", by) for by in STEPS]

    own, give, wa = early_project([mine, *near, other], mods, wa, wb)
    pair0 = [g.reshape(-1, rows, g.shape[-1]) for g in (own, around(give, "core", 1))]
    state = early(*pair0)
    own, give = project(far, mods, wa, wb)
    pair1 = [g.reshape(-1, rows, g.shape[-1]) for g in (own, around(give, "core", 1))]

    pair, third, first3, last3 = attend(pair0 + pair1, state)
    before = along(last3, 1)
    after = along(first3, -1)
    avg = average(overlap, place, pair, third, before, after)
    avg = lax.all_to_all(avg, ("x", "yhi", "core"), 0, 0)
    return blend(mine, mods, avg).reshape(latents.shape)


def solution(mesh):
    fine = Mesh(mesh.devices.reshape(4, 8, NX, NY, NC), ("ylo", "z", "x", "yhi", "core"))
    win, head = ("ylo", "z"), ("x", "yhi", "core")
    in_specs = (P(win, None, head, None), P(win), P(), P(None, head, None), P())
    out_specs = P(win, None, head, None)
    return jax.shard_map(shards, mesh=fine, in_specs=in_specs, out_specs=out_specs, check_vma=False)
```

```python
import functools

import jax
import jax.numpy as jnp
from jax import lax
from jax.experimental import pallas as pl
from jax.experimental.pallas import tpu as pltpu
from jax.sharding import Mesh
from jax.sharding import PartitionSpec as P

HEAD_DIM = 64
OMAX = 3
NX, NY, NC = 4, 2, 2
MIB = 1 << 20
STEPS = (2, 1, 3)
ORIGINS = tuple((NX - by) % NX for by in STEPS)
SUM_LANE, TOP_LANE = HEAD_DIM, HEAD_DIM + 1
PATCH = 8


def cost(flops, inputs, outputs, transcendentals=0):
    size = sum(a.size * a.dtype.itemsize for a in (*inputs, *outputs))
    return pl.CostEstimate(flops=flops, bytes_accessed=size, transcendentals=transcendentals)


def choose_kernel(pid, source, out, modulation, sem):
    copy = pltpu.make_async_copy(source, modulation, sem)
    copy.start()
    copy.wait()
    for c in range(out.shape[0]):
        out[c : c + 1, :] = modulation[c, pl.ds(pid[0], 1), :]


def choose(pid, modulation):
    modulation = pltpu.with_memory_space_constraint(modulation, pltpu.HBM)
    return pl.pallas_call(
        choose_kernel,
        in_specs=[pl.BlockSpec(memory_space=pltpu.SMEM), pl.BlockSpec(memory_space=pltpu.HBM)],
        out_specs=pl.BlockSpec(memory_space=pltpu.VMEM),
        scratch_shapes=[pltpu.VMEM(modulation.shape, jnp.float32), pltpu.SemaphoreType.DMA],
        out_shape=jax.ShapeDtypeStruct((modulation.shape[0], modulation.shape[2]), jnp.float32),
        cost_estimate=cost(10**11, (), ()),
        compiler_params=pltpu.CompilerParams(vmem_limit_bytes=8 * MIB),
    )(pid, modulation)


def normalise(tokens, mods, normed, order, before):
    rows = tokens[-1].shape[0]
    shift = mods[0:1, :]
    scale = 1.0 + mods[1:2, :]
    for i in order:
        before(i)
        xf = tokens[i][...].astype(jnp.float32)
        mean = jnp.mean(xf, axis=-1, keepdims=True)
        xc = xf - mean
        var = jnp.mean(xc * xc, axis=-1, keepdims=True)
        normed[i * rows : (i + 1) * rows] = (xc * lax.rsqrt(var + 1e-06) * scale + shift).astype(jnp.bfloat16)


def product(normed, w, out):
    r = lax.dot_general(normed[...], w[...], (((1,), (1,)), ((), ())), preferred_element_type=jnp.float32)
    out[...] = r[: out.shape[0]].astype(jnp.bfloat16)


def early_project_kernel(blocks, *refs):
    tokens, (mods, wa, wb, oa, ob, va, first, normed, sems) = list(refs[:blocks]), refs[blocks:]
    head = pltpu.make_async_copy(tokens[0], first, sems.at[0])
    fetch = pltpu.make_async_copy(wa, va, sems.at[1])
    head.start()
    fetch.start()
    tokens[0] = first
    normalise(tokens, mods, normed, (*range(1, blocks), 0), lambda i: head.wait() if i == 0 else None)
    product(normed, wb, ob)
    fetch.wait()
    product(normed, va, oa)


def early_project(blocks, mods, wa, wb):
    rows = sum(b.shape[0] for b in blocks)
    feats, width = wa.shape
    full = pl.BlockSpec(memory_space=pltpu.VMEM)
    away = pl.BlockSpec(memory_space=pltpu.HBM)
    first, wa = [pltpu.with_memory_space_constraint(a, pltpu.HBM) for a in (blocks[0], wa)]
    shape = jax.ShapeDtypeStruct((rows, feats), jnp.bfloat16)
    weight = jax.ShapeDtypeStruct((feats, width), jnp.bfloat16)
    return pl.pallas_call(
        functools.partial(early_project_kernel, len(blocks)),
        in_specs=[away] + [full] * len(blocks) + [away, full],
        out_specs=[full] * 3,
        out_shape=[shape, shape, weight],
        scratch_shapes=[
            pltpu.VMEM(first.shape, jnp.bfloat16),
            pltpu.VMEM((rows, width), jnp.bfloat16),
            pltpu.SemaphoreType.DMA((2,)),
        ],
        cost_estimate=cost(1, (), ()),
        compiler_params=pltpu.CompilerParams(vmem_limit_bytes=24 * MIB),
    )(first, *blocks[1:], mods, wa, wb)


def project_kernel(blocks, *refs):
    tokens, (mods, wa, wb, oa, ob, normed) = refs[:blocks], refs[blocks:]
    used = oa.shape[0]
    if used < normed.shape[0]:
        normed[used:] = jnp.zeros((normed.shape[0] - used, normed.shape[1]), jnp.bfloat16)
    normalise(tokens, mods, normed, range(blocks), lambda i: None)
    product(normed, wb, ob)
    product(normed, wa, oa)


def project(blocks, mods, wa, wb):
    rows = sum(b.shape[0] for b in blocks)
    feats, width = wa.shape
    full = pl.BlockSpec(memory_space=pltpu.VMEM)
    shape = jax.ShapeDtypeStruct((rows, feats), jnp.bfloat16)
    return pl.pallas_call(
        functools.partial(project_kernel, len(blocks)),
        in_specs=[full] * (len(blocks) + 3),
        out_specs=[full] * 2,
        out_shape=[shape] * 2,
        scratch_shapes=[pltpu.VMEM((4 * blocks[0].shape[0], width), jnp.bfloat16)],
        cost_estimate=cost(1, (wa, wb), ()),
        compiler_params=pltpu.CompilerParams(vmem_limit_bytes=24 * MIB),
    )(*blocks, mods, wa, wb)


def columns(groups, part, h, rows=slice(None)):
    width = groups[0].shape[2] // 3
    a = part * width + h * HEAD_DIM
    taken = [g[:, rows, a : a + HEAD_DIM] for g in groups]
    return jnp.concatenate([t.reshape(-1, HEAD_DIM) for t in taken], axis=0)


def values(groups, h):
    v = columns(groups, 2, h)
    lane = lax.broadcasted_iota(jnp.int32, (v.shape[0], 2 * HEAD_DIM), 1)
    return jnp.where(lane == SUM_LANE, jnp.ones_like(v[:1, :1]), jnp.concatenate([v, jnp.zeros_like(v)], axis=1))


def scored(q, k):
    return lax.dot_general(q, k, (((1,), (1,)), ((), ())), preferred_element_type=jnp.float32)


def weighted(s, top, v):
    p = jnp.exp((s - top) * (HEAD_DIM**-0.5)).astype(jnp.bfloat16)
    return lax.dot_general(p, v, (((1,), (0,)), ((), ())), preferred_element_type=jnp.float32)


def early_kernel(own, got, state):
    groups = (own, got)
    lane = lax.broadcasted_iota(jnp.int32, (1, 2 * HEAD_DIM), 1)
    heads = own.shape[2] // 3 // HEAD_DIM
    s = scored(columns(groups, 0, 0), columns(groups, 1, 0))
    for h in range(heads):
        then = scored(columns(groups, 0, h + 1), columns(groups, 1, h + 1)) if h + 1 < heads else None
        top = jnp.max(s, axis=-1, keepdims=True)
        out = jnp.where(lane == TOP_LANE, top, weighted(s, top, values(groups, h)))
        state[:, :, 2 * h * HEAD_DIM : 2 * (h + 1) * HEAD_DIM] = out.reshape(-1, own.shape[1], 2 * HEAD_DIM)
        s = then


def early(own, got):
    blocks, rows, feats = own.shape
    full = pl.BlockSpec(memory_space=pltpu.VMEM)
    shape = jax.ShapeDtypeStruct((2 * blocks, rows, feats // 3 * 2), jnp.float32)
    scores = (2 * blocks * rows) ** 2 * (feats // 3 // HEAD_DIM)
    return pl.pallas_call(
        early_kernel,
        in_specs=[full] * 2,
        out_specs=full,
        out_shape=shape,
        cost_estimate=cost(1, (), ()),
        compiler_params=pltpu.CompilerParams(vmem_limit_bytes=24 * MIB),
    )(own, got)


def attend_kernel(own0, got0, own1, got1, state, pair, third, first3, last3):
    a, b = (own0, got0), (own1, got1)
    rows = own0.shape[1]
    heads = own0.shape[2] // 3 // HEAD_DIM
    jobs = [(h, late) for h in range(heads) for late in (False, True)]

    def score(h, late):
        k = columns(b, 1, h)
        if late:
            return scored(columns(b, 0, h), jnp.concatenate([columns(a, 1, h), k], axis=0))
        return scored(columns(a, 0, h), k)

    done = {}
    s = score(*jobs[0])
    for i, (h, late) in enumerate(jobs):
        then = score(*jobs[i + 1]) if i + 1 < len(jobs) else None
        v = values(b, h)
        if late:
            top = jnp.max(s, axis=-1, keepdims=True)
            o = weighted(s, top, jnp.concatenate([values(a, h), v], axis=0))
        else:
            before = state[:, :, 2 * h * HEAD_DIM : 2 * (h + 1) * HEAD_DIM].reshape(-1, 2 * HEAD_DIM)
            top0 = before[:, TOP_LANE : TOP_LANE + 1]
            top = jnp.maximum(top0, jnp.max(s, axis=-1, keepdims=True))
            o = before * jnp.exp((top0 - top) * (HEAD_DIM**-0.5)) + weighted(s, top, v)
        done[h, late] = (o[:, :HEAD_DIM] / o[:, SUM_LANE : SUM_LANE + 1]).reshape(2, -1, rows, HEAD_DIM)
        s = then
    out = []
    for h in range(heads):
        parts = [done[h, late][j] for j in range(2) for late in (False, True)]
        out.append(jnp.concatenate(parts, axis=0))
    two = jnp.concatenate(out[:2], axis=2)
    pair[...] = two.astype(jnp.bfloat16)
    third[...] = out[2].astype(jnp.bfloat16)
    edge = OMAX * PATCH
    half = two.shape[0] // 2
    for ref, at in ((first3, 0), (last3, rows - edge)):
        cut = slice(at, at + edge)
        ref[: 2 * half * edge] = two[:, cut].reshape(-1, 2 * HEAD_DIM).astype(jnp.bfloat16)
        one = out[2][:, cut]
        one = jnp.concatenate([one[:half], one[half:]], axis=2)
        ref[2 * half * edge :] = one.reshape(-1, 2 * HEAD_DIM).astype(jnp.bfloat16)


def attend(groups, state):
    blocks = sum(g.shape[0] for g in groups)
    _, rows, feats = groups[0].shape
    full = pl.BlockSpec(memory_space=pltpu.VMEM)
    edge = blocks * OMAX * PATCH * 3 // 2
    shapes = [
        jax.ShapeDtypeStruct(s, jnp.bfloat16)
        for s in ((blocks, rows, 2 * HEAD_DIM), (blocks, rows, HEAD_DIM), (edge, 2 * HEAD_DIM), (edge, 2 * HEAD_DIM))
    ]
    return pl.pallas_call(
        attend_kernel,
        in_specs=[full] * 5,
        out_specs=[full] * 4,
        out_shape=shapes,
        compiler_params=pltpu.CompilerParams(vmem_limit_bytes=32 * MIB),
    )(*groups, state)


def unpacked(ref, blocks):
    rows = OMAX * PATCH
    data = ref[...].astype(jnp.float32)
    two = data[: blocks * rows].reshape(blocks, rows, 2 * HEAD_DIM)
    one = data[blocks * rows :].reshape(blocks // 2, rows, 2 * HEAD_DIM)
    return two, jnp.concatenate([one[:, :, :HEAD_DIM], one[:, :, HEAD_DIM:]], axis=0)


def average_kernel(overlap, place, pair, third, before, after, out):
    blocks, rows, _ = pair.shape
    frames = rows // PATCH
    ov_prev, ov_next = overlap[0], overlap[1]
    whole = []
    for mine, prev, nxt in zip((pair, third), unpacked(before, blocks), unpacked(after, blocks)):
        mine = mine[...].astype(jnp.float32)
        done = []
        for f in range(frames):
            cur = mine[:, f * PATCH : (f + 1) * PATCH]
            if f < OMAX or f >= frames - OMAX:
                if f < OMAX:
                    shared, source, at = f < ov_prev, prev, OMAX - ov_prev + f
                else:
                    shared, source, at = f >= frames - ov_next, nxt, f - frames + ov_next
                part = jnp.zeros_like(cur)
                for j in range(OMAX):
                    part = jnp.where(shared & (at == j), source[:, j * PATCH : (j + 1) * PATCH], part)
                cur = (cur + part) * jnp.where(shared, 0.5, 1.0)
            done.append(cur)
        whole.append(done)
    two = jnp.concatenate(whole[0], axis=1).astype(jnp.bfloat16)
    half = frames // 2
    one = jnp.concatenate(
        [jnp.concatenate(whole[1][:half], axis=1), jnp.concatenate(whole[1][half:], axis=1)], axis=2
    ).astype(jnp.bfloat16)
    for n in range(blocks):
        i = n % (blocks // 2)
        x = lax.rem(place[0] + (0, *ORIGINS, 0, *ORIGINS)[i], NX)
        y = place[1] if i < NX else 1 - place[1]
        c = place[2] if n < blocks // 2 else 1 - place[2]
        h = (x * NY + y) * NC + c
        out[h, :rows] = two[n]
        out[h, rows:] = one[n]


def average(overlap, place, pair, third, before, after):
    full = pl.BlockSpec(memory_space=pltpu.VMEM)
    smem = pl.BlockSpec(memory_space=pltpu.SMEM)
    blocks, rows, lanes = pair.shape
    return pl.pallas_call(
        average_kernel,
        in_specs=[smem] * 2 + [full] * 4,
        out_specs=full,
        out_shape=jax.ShapeDtypeStruct((blocks, rows * 3 // 2, lanes), jnp.bfloat16),
        compiler_params=pltpu.CompilerParams(vmem_limit_bytes=16 * MIB),
    )(overlap, place, pair, third, before, after)


def blend_kernel(lat, mods, avg, out):
    blocks = avg.shape[0]
    rows = lat.shape[0]
    width = 3 * HEAD_DIM
    for b in range(0, blocks, 2):
        parts = []
        for s in (b, b + 1):
            parts.append(avg[s, :rows].astype(jnp.float32))
            one = avg[s, rows:].astype(jnp.float32)
            parts.append(jnp.concatenate([one[:, :HEAD_DIM], one[:, HEAD_DIM:]], axis=0))
        cols = slice(b * width, (b + 2) * width)
        a = jnp.concatenate(parts, axis=1)
        out[:, cols] = (lat[:, cols].astype(jnp.float32) + mods[2:3, cols] * a).astype(jnp.bfloat16)


def blend(lat, mods, avg):
    full = pl.BlockSpec(memory_space=pltpu.VMEM)
    return pl.pallas_call(
        blend_kernel,
        in_specs=[full] * 3,
        out_specs=full,
        out_shape=jax.ShapeDtypeStruct(lat.shape, jnp.bfloat16),
        compiler_params=pltpu.CompilerParams(vmem_limit_bytes=16 * MIB),
    )(lat, mods, avg)


def around(value, axis, by):
    n = lax.axis_size(axis)
    return lax.ppermute(value, axis, [(i, (i + by) % n) for i in range(n)])


def along(value, by):
    n = lax.axis_size(("ylo", "z"))
    return lax.ppermute(value, ("ylo", "z"), [(i, i + by) for i in range(n) if 0 <= i + by < n])


def shards(latents, prompt_ids, modulation, w_qkv, intersection):
    _, frames, patches, width = latents.shape
    rows = frames * patches
    mine = latents.reshape(rows, width)
    wa = w_qkv.reshape(-1, width)
    place = jnp.stack([lax.axis_index("x"), lax.axis_index("yhi"), lax.axis_index("core")]).astype(jnp.int32)

    mods = choose(prompt_ids, jnp.transpose(modulation, (1, 0, 2)))
    window = lax.axis_index(("ylo", "z"))
    padded = jnp.concatenate([intersection, jnp.zeros((1,), jnp.int32)])
    overlap = lax.dynamic_slice(padded, (window,), (2,))

    other = around(mine, "yhi", 1)
    near = [around(mine, "x", by) for by in STEPS]
    wb = around(wa, "core", 1)
    far = [around(other, "x", by) for by in STEPS]

    own, give, wa = early_project([mine, *near], mods, wa, wb)
    pair0 = [g.reshape(-1, rows, g.shape[-1]) for g in (own, around(give, "core", 1))]
    state = early(*pair0)
    own, give = project([other, *far], mods, wa, wb)
    pair1 = [g.reshape(-1, rows, g.shape[-1]) for g in (own, around(give, "core", 1))]

    pair, third, first3, last3 = attend(pair0 + pair1, state)
    before = along(last3, 1)
    after = along(first3, -1)
    avg = average(overlap, place, pair, third, before, after)
    avg = lax.all_to_all(avg, ("x", "yhi", "core"), 0, 0)
    return blend(mine, mods, avg).reshape(latents.shape)


def solution(mesh):
    fine = Mesh(mesh.devices.reshape(4, 8, NX, NY, NC), ("ylo", "z", "x", "yhi", "core"))
    win, head = ("ylo", "z"), ("x", "yhi", "core")
    in_specs = (P(win, None, head, None), P(win), P(), P(None, head, None), P())
    out_specs = P(win, None, head, None)
    return jax.shard_map(shards, mesh=fine, in_specs=in_specs, out_specs=out_specs, check_vma=False)
```
